128 devices in a mesh: grp: 8 (over z, x_lo), dev: 16 (over y, x_hi, core).
Axes of the slice: x: 4 (x_hi: 2, x_lo: 2; x = x_hi * 2 + x_lo), y: 4, z: 4, core: 2. Of those that a mesh axis runs over, the one named last changes fastest.
Arguments:
- homolog_hidden_states: bfloat16 [512, 1024, 256], P(None, ('grp', 'dev')), may hold values from -6 to 6
- homolog_presence_marks: int32 [1024, 512], P(('grp', 'dev')), may hold values from 0 to 1, as said below
- prior_layernorm_scale: float32 [256], replicated, may hold values from 0.1 to 1.9
- prior_layernorm_shift: float32 [256], replicated, may hold values from -0.625 to 0.625
- former_embedding_weights: bfloat16 [256, 32], replicated, may hold values from -0.375 to 0.375
- former_embedding_shift: float32 [32], replicated, may hold values from -0.625 to 0.625
- latter_embedding_weights: bfloat16 [256, 32], replicated, may hold values from -0.375 to 0.375
- latter_embedding_shift: float32 [32], replicated, may hold values from -0.625 to 0.625
- dyadic_combiner_weights: bfloat16 [1024, 128], replicated, may hold values from -1.5 to 1.5
- lineward_layernorm_scale: float32 [256], replicated, may hold values from 0.1 to 1.9
- lineward_layernorm_shift: float32 [256], replicated, may hold values from -1.25 to 1.25
Outputs:
- pair_state_update: bfloat16 [1024, 8, 128, 128], P('grp', None, 'dev')
- alignment_row_split: bfloat16 [512, 1024, 256], P(('grp', 'dev'))
The draws below stay inside these ranges and needn't reach their ends.
Inputs may be any that keep to these rules, and one draw needn't show every extreme that they name: `homolog_presence_marks`: entry [i, 0] (the query sequence) is 1 for every residue i; each residue's other rows are present at a rate of its own.
All inputs are finite; a program needn't handle non-finite values.
Results may differ from the reference program's by a relative error of at most 0.0075.
Values may be sent and summed in bfloat16 or wider, within the bound.
A program may use at most 192 MiB of HBM per device.

```python
import jax
import jax.numpy as jnp
from jax import lax

HOMOLOG_WIDTH = 256
PROJECTOR_WIDTH = 32
C_PAIR = 128
DEVICE_SITES = 8
PROTEIN_LENGTH = 1024
HOMOLOG_DEPTH = 512
RES_GRP = 128
N_GRP = 8


def draw_homolog_presence_marks(key, part):
    key = jax.random.fold_in(key, 11)
    depth_key, element_seed = jax.random.split(key)
    depth = jax.random.randint(depth_key, (PROTEIN_LENGTH, 1), 2, 17)
    element_collection = jax.random.randint(element_seed, (PROTEIN_LENGTH, HOMOLOG_DEPTH), 0, 16)
    present = (element_collection < depth).astype(jnp.int32)
    asked_line_ordinal = jnp.arange(HOMOLOG_DEPTH)[None, :] == 0
    return jnp.where(asked_line_ordinal, 1, present).astype(jnp.int32)


def levels(key, shape, cuts, smallest, top_value):
    loudness, own = 1.0, jax.random.fold_in(key, 6)
    for dim, blocks in cuts:
        heights = jnp.exp(jax.random.uniform(jax.random.fold_in(own, dim), (blocks,), jnp.float32, smallest / len(cuts), top_value / len(cuts)))
        loudness = loudness * jnp.repeat(heights, shape[dim] // blocks).reshape([-1 if axis == dim else 1 for axis in range(len(shape))])
    return loudness


def scatter_about(rng, dims, scale, limit, cuts=(), kind=jnp.bfloat16):
    result = scale * jax.random.normal(rng, dims, jnp.float32)
    if cuts:
        result = result * levels(rng, dims, cuts, -0.22, 0.18)
    return jnp.clip(result, -limit, limit).astype(kind)


def setup_inputs(seed: int = 0) -> dict:
    streams_of = jax.random.split(jax.random.key(seed), 12)
    homolog_hidden_states = scatter_about(streams_of[0], (HOMOLOG_DEPTH, PROTEIN_LENGTH, HOMOLOG_WIDTH), 1.0, 6.0, ((1, 128),))
    homolog_presence_marks = draw_homolog_presence_marks(jax.random.fold_in(streams_of[11], 71), 0)
    prior_layernorm_scale = jnp.clip(1.0 + 0.18 * jax.random.normal(streams_of[2], (HOMOLOG_WIDTH,), jnp.float32), 0.1, 1.9)
    prior_layernorm_shift = scatter_about(streams_of[3], (HOMOLOG_WIDTH,), 0.1, 0.625, (), jnp.float32)
    former_embedding_weights = scatter_about(streams_of[4], (HOMOLOG_WIDTH, PROJECTOR_WIDTH), HOMOLOG_WIDTH ** -0.5, 0.375)
    former_embedding_shift = scatter_about(streams_of[5], (PROJECTOR_WIDTH,), 0.1, 0.625, (), jnp.float32)
    latter_embedding_weights = scatter_about(streams_of[6], (HOMOLOG_WIDTH, PROJECTOR_WIDTH), HOMOLOG_WIDTH ** -0.5, 0.375)
    latter_embedding_shift = scatter_about(streams_of[7], (PROJECTOR_WIDTH,), 0.1, 0.625, (), jnp.float32)
    dyadic_combiner_weights = scatter_about(streams_of[8], (PROJECTOR_WIDTH * PROJECTOR_WIDTH, C_PAIR), 0.25, 1.5)
    lineward_layernorm_scale = jnp.clip(1.0 + 0.18 * jax.random.normal(streams_of[9], (HOMOLOG_WIDTH,), jnp.float32), 0.1, 1.9)
    lineward_layernorm_shift = scatter_about(streams_of[10], (HOMOLOG_WIDTH,), 0.2, 1.25, (), jnp.float32)
    return dict(homolog_hidden_states=homolog_hidden_states, homolog_presence_marks=homolog_presence_marks, prior_layernorm_scale=prior_layernorm_scale, prior_layernorm_shift=prior_layernorm_shift, former_embedding_weights=former_embedding_weights, former_embedding_shift=former_embedding_shift, latter_embedding_weights=latter_embedding_weights, latter_embedding_shift=latter_embedding_shift, dyadic_combiner_weights=dyadic_combiner_weights, lineward_layernorm_scale=lineward_layernorm_scale, lineward_layernorm_shift=lineward_layernorm_shift)


def standardize_features(homolog_hidden_states):
    collected_numbers = homolog_hidden_states.astype(jnp.float32)
    average = lax.optimization_barrier(jnp.mean(collected_numbers, axis=-1, keepdims=True))
    centered = collected_numbers - average
    variance = lax.optimization_barrier(jnp.mean(centered * centered, axis=-1, keepdims=True))
    return centered * lax.rsqrt(variance + 1e-05)

def project(normed, weight, bias, cover_full_width):
    product = jnp.einsum('src,ce->res', normed.astype(jnp.float32), weight.astype(jnp.float32))
    return ((product + bias[None, :, None]) * cover_full_width[:, None, :]).astype(jnp.bfloat16)

def pair_block(initial_mapped_lines, left_mask, right_rows, right_mask, dyadic_combiner_weights):
    count_i = initial_mapped_lines.shape[0]
    count_j = right_rows.shape[0]
    width = initial_mapped_lines.shape[1]
    depth = initial_mapped_lines.shape[2]
    outer = jnp.dot(initial_mapped_lines.reshape(count_i * width, depth), right_rows.reshape(count_j * width, depth).T, preferred_element_type=jnp.float32)
    outer = outer.astype(jnp.bfloat16).reshape(count_i, width, count_j, width)
    outer = outer.transpose(0, 2, 1, 3).reshape(count_i * count_j, width * width)
    linear = jnp.dot(outer, dyadic_combiner_weights, preferred_element_type=jnp.float32).reshape(count_i, count_j, -1)
    count = jnp.dot(left_mask, right_mask.T, preferred_element_type=jnp.float32)
    return linear / (count + 0.001)[:, :, None]

def reference(homolog_hidden_states, homolog_presence_marks, prior_layernorm_scale, prior_layernorm_shift, former_embedding_weights, former_embedding_shift, latter_embedding_weights, latter_embedding_shift, dyadic_combiner_weights, lineward_layernorm_scale, lineward_layernorm_shift):
    averaged_outer_tensor = standardize_features(homolog_hidden_states)
    normed = (averaged_outer_tensor * prior_layernorm_scale + prior_layernorm_shift).astype(jnp.bfloat16)
    alignment_row_split = (averaged_outer_tensor * lineward_layernorm_scale + lineward_layernorm_shift).astype(jnp.bfloat16)
    cover_full_width = homolog_presence_marks.astype(jnp.float32)
    cover_half_width = homolog_presence_marks.astype(jnp.bfloat16)
    initial_mapped_lines = project(normed, former_embedding_weights, former_embedding_shift, cover_full_width)
    right_rows = project(normed, latter_embedding_weights, latter_embedding_shift, cover_full_width)
    tile_collection = PROTEIN_LENGTH // DEVICE_SITES
    leading_tile_collection = initial_mapped_lines.reshape(tile_collection, DEVICE_SITES, PROJECTOR_WIDTH, HOMOLOG_DEPTH)
    cover_tile_collection = cover_half_width.reshape(tile_collection, DEVICE_SITES, HOMOLOG_DEPTH)

    def one_block(items):
        return pair_block(items[0], items[1], right_rows, cover_half_width, dyadic_combiner_weights).astype(jnp.bfloat16)
    pair_rows = lax.map(one_block, (leading_tile_collection, cover_tile_collection))
    pair_state_update = pair_rows.reshape(PROTEIN_LENGTH, N_GRP, RES_GRP, C_PAIR)
    return (pair_state_update, alignment_row_split)
```

```python
import jax
import jax.numpy as jnp
from jax import lax
from jax.experimental import pallas as pl
from jax.experimental.pallas import tpu as pltpu
from jax.sharding import PartitionSpec as P

MESH = pl.DeviceIdType.MESH
F32 = jnp.float32
BF16 = jnp.bfloat16

SEQ = 512
SITES = 8
WIDTH = 256
PROJ = 32
PAIR = 128
NDEV = 128
CHUNK = 32
NCHUNK = SEQ // CHUNK
BLOCK = SITES * PROJ
SLOT = BLOCK + 16
MIX = 85


def place():
    g = lax.axis_index("grp")
    d = lax.axis_index("dev")
    return g, d


def coords(g, d):
    return (d // 2 % 2) * 2 + g % 2, d // 4, g // 2, d % 2


def remote(src, dst, send, recv, target):
    return pltpu.make_async_remote_copy(
        src_ref=src, dst_ref=dst, send_sem=send, recv_sem=recv, device_id=target, device_id_type=MESH
    )


def column(row):
    n = row.shape[1]
    a = lax.broadcasted_iota(jnp.int32, (n, n), 0)
    b = lax.broadcasted_iota(jnp.int32, (n, n), 1)
    return jnp.sum(jnp.where(a == b, jnp.broadcast_to(row, (n, n)), 0.0), axis=1, keepdims=True)


def kernel(
    x_hbm, marks, gain1, shift1, wl, bl, wr, br, wd, gain2, shift2,
    pair_hbm, row_hbm,
    xv, nf, rowbuf, rf, lslot, rslot, ra, rt, mrt, wf, w2, xs, outv,
    xsem, lrecv, lsend, rrecv, rsend, asend, arecv, osem,
):
    g, d = place()
    me = g * 16 + d
    x0, y0, z0, c0 = coords(g, d)
    xh0 = d // 2 % 2

    def peer(k):
        m = lax.rem(k * MIX, NDEV)
        x = (x0 + m) % 4
        y = (y0 + m // 4) % 4
        z = (z0 + m // 16) % 4
        c = (c0 + m // 64) % 2
        return z * 2 + x % 2, y * 4 + (x // 2) * 2 + c

    def xcopy(k):
        return pltpu.make_async_copy(
            x_hbm.at[pl.ds(k * CHUNK, CHUNK)], xv.at[pl.ds(k * CHUNK, CHUNK)], xsem.at[k]
        )

    for k in range(NCHUNK):
        xcopy(k).start()

    barrier = pltpu.get_barrier_semaphore()

    def greet(k, carry):
        pl.semaphore_signal(barrier, inc=1, device_id=peer(k), device_id_type=MESH)
        return carry

    lax.fori_loop(1, NDEV, greet, 0)

    def norm(k, carry):
        xcopy(k).wait()
        x = xv[pl.ds(k * CHUNK, CHUNK)].astype(F32).reshape(CHUNK * SITES, WIDTH)
        mean = jnp.sum(x, axis=-1, keepdims=True) * (1.0 / WIDTH)
        cen = x - mean
        var = jnp.sum(cen * cen, axis=-1, keepdims=True) * (1.0 / WIDTH)
        scaled = cen * lax.rsqrt(var + 1e-05)
        rows = pl.ds(pl.multiple_of(k * CHUNK * SITES, CHUNK * SITES), CHUNK * SITES)
        rowbuf[rows, :] = (scaled * gain2[...] + shift2[...]).astype(BF16)
        normed = scaled * gain1[...] + shift1[...]
        nf[0, rows, :] = normed[:, :128]
        nf[1, rows, :] = normed[:, 128:]
        return carry

    lax.fori_loop(0, NCHUNK, norm, 0)

    wt = jnp.concatenate([wl[...], wr[...]], axis=0)
    bias = jnp.concatenate([column(bl[...]), column(br[...])], axis=0)
    mask = marks[...].astype(F32)
    mask16 = jnp.concatenate([mask, jnp.zeros_like(mask)], axis=0).astype(BF16)
    for i in range(SITES):
        rows = jnp.concatenate(
            [nf[0, pl.ds(i, SEQ, stride=SITES), :], nf[1, pl.ds(i, SEQ, stride=SITES), :]], axis=1
        ).astype(BF16)
        p = lax.dot_general(wt, rows, (((1,), (1,)), ((), ())), preferred_element_type=F32)
        p = (p + bias) * mask[i : i + 1, :]
        lslot[d, pl.ds(i * PROJ, PROJ), :] = p[:PROJ].astype(BF16)
        for h in range(4):
            rf[h, pl.ds(i, PROJ, stride=SITES), :] = p[PROJ:, h * 128 : (h + 1) * 128]
    for h in range(4):
        rslot[g, pl.ds(0, BLOCK), pl.ds(h * 128, 128)] = rf[h].astype(BF16)
    lslot[d, pl.ds(BLOCK, 16), :] = mask16
    rslot[g, pl.ds(BLOCK, 16), :] = mask16

    pl.semaphore_wait(barrier, NDEV - 1)

    def lcopy(slot, target):
        return remote(lslot.at[slot], lslot.at[slot], lsend, lrecv.at[slot], target)

    def rcopy(slot, target):
        return remote(rslot.at[slot], rslot.at[slot], rsend, rrecv.at[slot], target)

    def left_slot(dy, dxh, dc):
        return (y0 + dy) % 4 * 4 + (xh0 + dxh) % 2 * 2 + (c0 + dc) % 2

    def right_slot(dz, dxl):
        return (z0 + dz) % 4 * 2 + (g + dxl) % 2

    sibling = (g, left_slot(0, 0, 1))
    lpartner = left_slot(0, 1, 0)
    rpartner = right_slot(0, 1)

    rcopy(g, (rpartner, d)).start()
    lcopy(d, (g, lpartner)).start()
    lcopy(d, sibling).start()
    for k in (1, 3, 2):
        rcopy(g, (right_slot(k, 0), d)).start()
        lcopy(d, (g, left_slot(k, 0, 0))).start()

    def send_row(k, carry):
        tg, td = peer(k)
        to = tg * 16 + td
        remote(
            rowbuf.at[pl.ds(pl.multiple_of(to * 32, 32), 32)],
            row_hbm.at[pl.ds(pl.multiple_of(me * 32, 32), 32)],
            asend, arecv, (tg, td),
        ).start()
        return carry

    mine = pl.ds(pl.multiple_of(me * 32, 32), 32)
    pltpu.make_async_copy(rowbuf.at[mine], row_hbm.at[mine], arecv).start()
    lax.fori_loop(1, 48, send_row, 0)

    rcopy(rpartner, (g, d)).wait_recv()
    for k in (1, 3, 2):
        rcopy(rpartner, (right_slot(k, 0), d)).start()
    lcopy(lpartner, (g, d)).wait_recv()
    for k in (1, 3, 2):
        lcopy(lpartner, (g, left_slot(k, 0, 0))).start()
    lcopy(lpartner, sibling).start()

    lax.fori_loop(48, NDEV, send_row, 0)

    wf[...] = wd[...].astype(F32)
    for e2 in range(2):
        stack = jnp.concatenate(
            [wf[pl.ds(2 * ep + e2, PROJ, stride=PROJ), :] for ep in range(PROJ // 2)], axis=0
        )
        w2[pl.ds(e2 * PAIR, PAIR), :] = stack.T.astype(BF16)

    for k in (1, 3, 2):
        rcopy(right_slot(k, 0), (g, d)).wait_recv()
        rcopy(right_slot(k, 1), (g, d)).wait_recv()

    def merge(t, carry):
        e = pl.multiple_of(t * 4 * SITES, 4 * SITES)
        for q in range(4):
            a = rslot[2 * q, pl.ds(e, 4 * SITES), :].astype(F32).reshape(4, SITES, SEQ)
            b = rslot[2 * q + 1, pl.ds(e, 4 * SITES), :].astype(F32).reshape(4, SITES, SEQ)
            ra[:, pl.ds(q * 16, 16), :] = jnp.concatenate([a, b], axis=1).astype(BF16)
        for h in range(2):
            block = ra[2 * h : 2 * h + 2].reshape(128, SEQ)
            lanes = pl.ds(pl.multiple_of(t * 256 + h * 128, 128), 128)
            rt[:, lanes] = block.T
        return carry

    lax.fori_loop(0, PROJ // 4, merge, 0)
    mr = jnp.concatenate(
        [rslot[k, pl.ds(BLOCK, 16), :].astype(F32)[:SITES] for k in range(8)], axis=0
    )
    mrt[...] = jnp.concatenate([mr, mr], axis=0).astype(BF16).T

    low = lax.broadcasted_iota(jnp.int32, (1, 128), 1) < 64

    def block(slot):
        lhs = lslot[slot, pl.ds(0, BLOCK), :]
        for nb in range(8):
            x = jnp.dot(lhs, rt[:, nb * 256 : (nb + 1) * 256], preferred_element_type=F32).astype(BF16)
            for h in range(2):
                ep = nb * 2 + h
                for i in range(SITES):
                    xs[i, ep * PROJ : (ep + 1) * PROJ, :] = x[
                        i * PROJ : (i + 1) * PROJ, h * 128 : (h + 1) * 128
                    ]
        count = jnp.dot(lslot[slot, pl.ds(BLOCK, 16), :], mrt[...], preferred_element_type=F32)
        inverse = 1.0 / (count + 0.001)
        for i in range(0, SITES, 2):
            rhs = jnp.concatenate([xs[i], xs[i + 1]], axis=1)
            y = jnp.dot(w2[...], rhs, preferred_element_type=F32)
            a, b = y[:PAIR], y[PAIR:]
            first = a[:, :128] + pltpu.roll(b[:, :128], 64, axis=1)
            second = b[:, 128:] + pltpu.roll(a[:, 128:], 64, axis=1)
            both = jnp.where(low, first, second)
            scale = jnp.where(low, inverse[i : i + 1], inverse[i + 1 : i + 2])
            at = pl.ds(pl.multiple_of(slot * 512 + i * 64, 128), 128)
            outv[at, :] = (both * scale).T.astype(BF16)
        at = pl.ds(pl.multiple_of(slot * 512, 512), 512)
        pltpu.make_async_copy(outv.at[at], pair_hbm.at[at], osem).start()

    def chip(t, carry):
        o = t // 2
        dy = o + (o // 2) * (5 - 2 * o)
        dxh = t % 2
        direct = left_slot(dy, dxh, 0)
        other = left_slot(dy, dxh, 1)

        @pl.when(t >= 2)
        def _():
            lcopy(direct, (g, d)).wait_recv()
            lcopy(direct, sibling).start()

        block(direct)
        lcopy(other, (g, d)).wait_recv()
        block(other)
        return carry

    lax.fori_loop(0, 8, chip, 0)

    pltpu.make_async_copy(lslot.at[pl.ds(0, 15)], lslot.at[pl.ds(0, 15)], lsend).wait()
    pltpu.make_async_copy(rslot.at[pl.ds(0, 7)], rslot.at[pl.ds(0, 7)], rsend).wait()
    rest = pl.ds(0, (NDEV - 1) * 32)
    pltpu.make_async_copy(rowbuf.at[rest], rowbuf.at[rest], asend).wait()
    pltpu.make_async_copy(rowbuf, row_hbm, arecv).wait()
    pltpu.make_async_copy(outv, pair_hbm, osem).wait()


def body(x, marks, gain1, shift1, wl, bl, wr, br, wd, gain2, shift2):
    vmem = pl.BlockSpec(memory_space=pltpu.VMEM)
    hbm = pl.BlockSpec(memory_space=pl.ANY)
    pair, rows = pl.pallas_call(
        kernel,
        out_shape=(
            jax.ShapeDtypeStruct((8192, PAIR), BF16),
            jax.ShapeDtypeStruct((NDEV * 32, WIDTH), BF16),
        ),
        in_specs=[hbm] + [vmem] * 10,
        out_specs=(hbm, hbm),
        scratch_shapes=[
            pltpu.VMEM((SEQ, SITES, WIDTH), BF16),
            pltpu.VMEM((2, SEQ * SITES, 128), F32),
            pltpu.VMEM((SEQ * SITES, WIDTH), BF16),
            pltpu.VMEM((4, BLOCK, 128), F32),
            pltpu.VMEM((16, SLOT, SEQ), BF16),
            pltpu.VMEM((8, SLOT, SEQ), BF16),
            pltpu.VMEM((4, 64, SEQ), BF16),
            pltpu.VMEM((SEQ, 2048), BF16),
            pltpu.VMEM((SEQ, 128), BF16),
            pltpu.VMEM((PROJ * PROJ, PAIR), F32),
            pltpu.VMEM((2 * PAIR, 512), BF16),
            pltpu.VMEM((SITES, 512, 128), BF16),
            pltpu.VMEM((8192, PAIR), BF16),
            pltpu.SemaphoreType.DMA((NCHUNK,)),
            pltpu.SemaphoreType.DMA((16,)),
            pltpu.SemaphoreType.DMA,
            pltpu.SemaphoreType.DMA((8,)),
            pltpu.SemaphoreType.DMA,
            pltpu.SemaphoreType.DMA,
            pltpu.SemaphoreType.DMA,
            pltpu.SemaphoreType.DMA,
        ],
        compiler_params=pltpu.CompilerParams(
            collective_id=0, has_side_effects=True, vmem_limit_bytes=48 << 20
        ),
    )(
        x, marks, gain1[None], shift1[None], wl.T, bl[None], wr.T, br[None], wd, gain2[None], shift2[None]
    )
    pair = pair.reshape(128, 8, 8, PAIR)
    rows = rows.reshape(NDEV, 4, SITES, WIDTH).transpose(1, 0, 2, 3).reshape(4, 1024, WIDTH)
    return pair, rows


def solution(mesh):
    everywhere = P()
    return jax.shard_map(
        body,
        mesh=mesh,
        in_specs=(P(None, ("grp", "dev"), None), P(("grp", "dev"), None)) + (everywhere,) * 9,
        out_specs=(P("grp", None, "dev", None), P(("grp", "dev"), None, None)),
        check_vma=False,
    )
```

```python
import jax
import jax.numpy as jnp
from jax import lax
from jax.experimental import pallas as pl
from jax.experimental.pallas import tpu as pltpu
from jax.sharding import PartitionSpec as P

MESH = pl.DeviceIdType.MESH
F32 = jnp.float32
BF16 = jnp.bfloat16

SEQ = 512
SITES = 8
WIDTH = 256
PROJ = 32
PAIR = 128
NDEV = 128
CHUNK = 128
NCHUNK = SEQ // CHUNK
BLOCK = SITES * PROJ
SLOT = BLOCK + 16
HALF = 128
B0, B1, B2 = 2, 3, 3


def place():
    g = lax.axis_index("grp")
    d = lax.axis_index("dev")
    return g, d


def coords(g, d):
    return (d // 2 % 2) * 2 + g % 2, d // 4, g // 2, d % 2


def remote(src, dst, send, recv, target):
    return pltpu.make_async_remote_copy(
        src_ref=src, dst_ref=dst, send_sem=send, recv_sem=recv, device_id=target, device_id_type=MESH
    )


def column(row):
    n = row.shape[1]
    a = lax.broadcasted_iota(jnp.int32, (n, n), 0)
    b = lax.broadcasted_iota(jnp.int32, (n, n), 1)
    return jnp.sum(jnp.where(a == b, jnp.broadcast_to(row, (n, n)), 0.0), axis=1, keepdims=True)


def kernel(
    x_hbm, marks_h, gain1_h, shift1_h, wl_h, bl_h, wr_h, br_h, wd_h, gain2_h, shift2_h,
    pair_hbm, row_hbm,
    marks, gain1, shift1, wl, bl, wr, br, wd, gain2, shift2,
    xv, nf, rowbuf, rf, lslot, rslot, ra, rt, mrt, wf, w2, xs, outv,
    psem, xsem, lrecv, lrecv2, lsend, rrecv, rrecv2, rsend, asend, arecv, osem, ready,
):
    g, d = place()
    me = g * 16 + d
    x0, y0, z0, c0 = coords(g, d)
    xh0 = d // 2 % 2

    groups = [
        (z0 + dz) % 4 * 2 + (g + dx) % 2 for dx, dz in
        ((0, 1), (1, 3), (0, 3), (1, 1), (0, 2), (1, 2), (1, 0), (0, 0))
    ]

    def column_of(q):
        o = lax.rem(q, 4)
        u = lax.rem(lax.div(q, 4) + 1, 4)
        dy = 1 + 2 * o + lax.div(o, 2) * (5 - 4 * o)
        return (
            lax.rem(y0 + dy, 4) * 4
            + lax.rem(xh0 + lax.div(u, 2), 2) * 2
            + lax.rem(c0 + lax.rem(u, 2), 2)
        )

    def xcopy(k):
        return pltpu.make_async_copy(
            x_hbm.at[pl.ds(k * CHUNK, CHUNK)], xv.at[pl.ds(k * CHUNK, CHUNK)], xsem.at[k]
        )

    small = (
        (gain1_h, gain1), (shift1_h, shift1), (gain2_h, gain2), (shift2_h, shift2), (marks_h, marks),
        (wl_h, wl), (wr_h, wr), (bl_h, bl), (br_h, br), (wd_h, wd),
    )
    for k, (a, b) in enumerate(small):
        pltpu.make_async_copy(a, b, psem.at[k]).start()
    for k in range(NCHUNK):
        xcopy(k).start()

    barrier = pltpu.get_barrier_semaphore()
    for tg in groups[:7]:
        pl.semaphore_signal(barrier, inc=1, device_id=(tg, d), device_id_type=MESH)
    for k in range(1, 16):
        pl.semaphore_signal(barrier, inc=1, device_id=(g, lax.rem(d + k, 16)), device_id_type=MESH)

    for k, (a, b) in enumerate(small):
        pltpu.make_async_copy(a, b, psem.at[k]).wait()

    def norm(k, carry):
        xcopy(k).wait()
        x = xv[pl.ds(k * CHUNK, CHUNK)].astype(F32).reshape(CHUNK * SITES, WIDTH)
        mean = jnp.sum(x, axis=-1, keepdims=True) * (1.0 / WIDTH)
        cen = x - mean
        var = jnp.sum(cen * cen, axis=-1, keepdims=True) * (1.0 / WIDTH)
        scaled = cen * lax.rsqrt(var + 1e-05)
        rows = pl.ds(pl.multiple_of(k * CHUNK * SITES, CHUNK * SITES), CHUNK * SITES)
        rowbuf[rows, :] = (scaled * gain2[...] + shift2[...]).astype(BF16)
        normed = scaled * gain1[...] + shift1[...]
        nf[0, rows, :] = normed[:, :128]
        nf[1, rows, :] = normed[:, 128:]
        return carry

    lax.fori_loop(0, NCHUNK // 2, norm, 0)

    pl.semaphore_wait(barrier, 22)
    for tg in groups[:7]:
        pl.semaphore_signal(ready, inc=1, device_id=(tg, d), device_id_type=MESH)

    lax.fori_loop(NCHUNK // 2, NCHUNK, norm, 0)

    pl.semaphore_wait(ready, 7)

    def send_rows(q, skip=0):
        td = column_of(q)
        for tg in groups[: 8 - skip]:
            to = tg * 16 + td
            remote(
                rowbuf.at[pl.ds(pl.multiple_of(to * 32, 32), 32)],
                row_hbm.at[pl.ds(pl.multiple_of(me * 32, 32), 32)],
                asend, arecv, (tg, td),
            ).start()

    def send_more(q, carry):
        send_rows(q)
        return carry

    mine = pl.ds(pl.multiple_of(me * 32, 32), 32)
    pltpu.make_async_copy(rowbuf.at[mine], row_hbm.at[mine], arecv).start()
    lax.fori_loop(0, B0, send_more, 0)

    wt = jnp.concatenate([wl[...], wr[...]], axis=0)
    bias = jnp.concatenate([column(bl[...]), column(br[...])], axis=0)
    mask = marks[...].astype(F32)
    mask16 = jnp.concatenate([mask, jnp.zeros_like(mask)], axis=0).astype(BF16)
    for i in range(SITES):
        rows = jnp.concatenate(
            [nf[0, pl.ds(i, SEQ, stride=SITES), :], nf[1, pl.ds(i, SEQ, stride=SITES), :]], axis=1
        ).astype(BF16)
        p = lax.dot_general(wt, rows, (((1,), (1,)), ((), ())), preferred_element_type=F32)
        p = (p + bias) * mask[i : i + 1, :]
        lslot[d, pl.ds(i * PROJ, PROJ), :] = p[:PROJ].astype(BF16)
        for h in range(4):
            rf[h, pl.ds(i, PROJ, stride=SITES), :] = p[PROJ:, h * 128 : (h + 1) * 128]
    for h in range(4):
        rslot[g, pl.ds(0, BLOCK), pl.ds(h * 128, 128)] = rf[h].astype(BF16)
    lslot[d, pl.ds(BLOCK, 16), :] = mask16
    rslot[g, pl.ds(BLOCK, 16), :] = mask16

    def lcopy(slot, target):
        return remote(lslot.at[slot], lslot.at[slot], lsend, lrecv.at[slot], target)

    def rcopy(slot, target):
        return remote(rslot.at[slot], rslot.at[slot], rsend, rrecv.at[slot], target)

    def left_slot(dy, dxh, dc):
        return (y0 + dy) % 4 * 4 + (xh0 + dxh) % 2 * 2 + (c0 + dc) % 2

    def right_slot(dz, dxl):
        return (z0 + dz) % 4 * 2 + (g + dxl) % 2

    sibling = (g, left_slot(0, 0, 1))
    lpartner = left_slot(0, 1, 0)
    rpartner = right_slot(0, 1)
    lup, ldown = (g, left_slot(1, 0, 0)), (g, left_slot(3, 0, 0))
    rup, rdown = (right_slot(1, 0), d), (right_slot(3, 0), d)
    first, second = pl.ds(0, HALF), pl.ds(HALF, SLOT - HALF)

    def lhalf(slot, part, sem, target):
        return remote(lslot.at[slot, part], lslot.at[slot, part], lsend, sem.at[slot], target)

    def rhalf(slot, part, sem, target):
        return remote(rslot.at[slot, part], rslot.at[slot, part], rsend, sem.at[slot], target)

    rcopy(g, (rpartner, d)).start()
    lcopy(d, (g, lpartner)).start()
    rcopy(g, rup).start()
    lcopy(d, lup).start()
    rcopy(g, rdown).start()
    lcopy(d, ldown).start()
    lcopy(d, sibling).start()

    lax.fori_loop(B0, B0 + B1, send_more, 0)

    rcopy(rpartner, (g, d)).wait_recv()
    rcopy(rpartner, rup).start()
    rcopy(rpartner, rdown).start()
    lcopy(lpartner, (g, d)).wait_recv()
    lcopy(lpartner, lup).start()
    lcopy(lpartner, ldown).start()
    lcopy(lpartner, sibling).start()

    def onward(k):
        low, high = right_slot(3, k), right_slot(1, k)
        rcopy(low, (g, d)).wait_recv()
        rhalf(low, first, rrecv, rup).start()
        rcopy(high, (g, d)).wait_recv()
        rhalf(high, second, rrecv2, rdown).start()
        low, high = left_slot(3, k, 0), left_slot(1, k, 0)
        lcopy(low, (g, d)).wait_recv()
        lhalf(low, first, lrecv, lup).start()
        lcopy(low, sibling).start()
        lcopy(high, (g, d)).wait_recv()
        lhalf(high, second, lrecv2, ldown).start()
        lcopy(high, sibling).start()

    onward(0)
    lax.fori_loop(B0 + B1, B0 + B1 + B2, send_more, 0)
    onward(1)

    wf[...] = wd[...].astype(F32)
    for e2 in range(2):
        stack = jnp.concatenate(
            [wf[pl.ds(2 * ep + e2, PROJ, stride=PROJ), :] for ep in range(PROJ // 2)], axis=0
        )
        w2[pl.ds(e2 * PAIR, PAIR), :] = stack.T.astype(BF16)

    for k in range(2):
        far = right_slot(2, k)
        rhalf(far, first, rrecv, (g, d)).wait_recv()
        rhalf(far, second, rrecv2, (g, d)).wait_recv()

    def merge(t, carry):
        e = pl.multiple_of(t * 4 * SITES, 4 * SITES)
        for q in range(4):
            a = rslot[2 * q, pl.ds(e, 4 * SITES), :].astype(F32).reshape(4, SITES, SEQ)
            b = rslot[2 * q + 1, pl.ds(e, 4 * SITES), :].astype(F32).reshape(4, SITES, SEQ)
            ra[:, pl.ds(q * 16, 16), :] = jnp.concatenate([a, b], axis=1).astype(BF16)
        for h in range(2):
            block = ra[2 * h : 2 * h + 2].reshape(128, SEQ)
            lanes = pl.ds(pl.multiple_of(t * 256 + h * 128, 128), 128)
            rt[:, lanes] = block.T
        return carry

    lax.fori_loop(0, PROJ // 4, merge, 0)
    mr = jnp.concatenate(
        [rslot[k, pl.ds(BLOCK, 16), :].astype(F32)[:SITES] for k in range(8)], axis=0
    )
    mrt[...] = jnp.concatenate([mr, mr], axis=0).astype(BF16).T

    low = lax.broadcasted_iota(jnp.int32, (1, 128), 1) < 64

    def block(slot):
        lhs = lslot[slot, pl.ds(0, BLOCK), :]
        for nb in range(8):
            x = jnp.dot(lhs, rt[:, nb * 256 : (nb + 1) * 256], preferred_element_type=F32).astype(BF16)
            for h in range(2):
                ep = nb * 2 + h
                for i in range(SITES):
                    xs[i, ep * PROJ : (ep + 1) * PROJ, :] = x[
                        i * PROJ : (i + 1) * PROJ, h * 128 : (h + 1) * 128
                    ]
        count = jnp.dot(lslot[slot, pl.ds(BLOCK, 16), :], mrt[...], preferred_element_type=F32)
        inverse = 1.0 / (count + 0.001)
        for i in range(0, SITES, 2):
            rhs = jnp.concatenate([xs[i], xs[i + 1]], axis=1)
            y = jnp.dot(w2[...], rhs, preferred_element_type=F32)
            a, b = y[:PAIR], y[PAIR:]
            early = a[:, :128] + pltpu.roll(b[:, :128], 64, axis=1)
            late = b[:, 128:] + pltpu.roll(a[:, 128:], 64, axis=1)
            both = jnp.where(low, early, late)
            scale = jnp.where(low, inverse[i : i + 1], inverse[i + 1 : i + 2])
            at = pl.ds(pl.multiple_of(slot * 512 + i * 64, 128), 128)
            outv[at, :] = (both * scale).T.astype(BF16)
        at = pl.ds(pl.multiple_of(slot * 512, 512), 512)
        pltpu.make_async_copy(outv.at[at], pair_hbm.at[at], osem).start()

    for k in range(2):
        far = left_slot(2, k, 0)
        lhalf(far, first, lrecv, (g, d)).wait_recv()
        lhalf(far, second, lrecv2, (g, d)).wait_recv()
        lcopy(far, sibling).start()

    def chip(t, carry):
        o = t // 2
        dy = o + (o // 2) * (5 - 2 * o)
        dxh = t % 2
        direct = left_slot(dy, dxh, 0)
        other = left_slot(dy, dxh, 1)

        @pl.when(t < 15 - B0 - B1 - B2)
        def _():
            send_rows(t + B0 + B1 + B2)

        block(direct)
        lcopy(other, (g, d)).wait_recv()
        block(other)
        return carry

    send_rows(15, 1)
    lax.fori_loop(0, 8, chip, 0)

    pltpu.make_async_copy(lslot.at[pl.ds(0, 15)], lslot.at[pl.ds(0, 15)], lsend).wait()
    pltpu.make_async_copy(rslot.at[pl.ds(0, 7)], rslot.at[pl.ds(0, 7)], rsend).wait()
    rest = pl.ds(0, (NDEV - 1) * 32)
    pltpu.make_async_copy(rowbuf.at[rest], rowbuf.at[rest], asend).wait()
    pltpu.make_async_copy(rowbuf, row_hbm, arecv).wait()
    pltpu.make_async_copy(outv, pair_hbm, osem).wait()


def body(x, marks, gain1, shift1, wl, bl, wr, br, wd, gain2, shift2):
    hbm = pl.BlockSpec(memory_space=pltpu.HBM)
    free = pl.BlockSpec(memory_space=pl.ANY)
    pair, rows = pl.pallas_call(
        kernel,
        out_shape=(
            jax.ShapeDtypeStruct((8192, PAIR), BF16),
            jax.ShapeDtypeStruct((NDEV * 32, WIDTH), BF16),
        ),
        in_specs=[hbm] * 11,
        out_specs=(free, free),
        scratch_shapes=[
            pltpu.VMEM((SITES, SEQ), jnp.int32),
            pltpu.VMEM((1, WIDTH), F32),
            pltpu.VMEM((1, WIDTH), F32),
            pltpu.VMEM((PROJ, WIDTH), BF16),
            pltpu.VMEM((1, PROJ), F32),
            pltpu.VMEM((PROJ, WIDTH), BF16),
            pltpu.VMEM((1, PROJ), F32),
            pltpu.VMEM((PROJ * PROJ, PAIR), BF16),
            pltpu.VMEM((1, WIDTH), F32),
            pltpu.VMEM((1, WIDTH), F32),
            pltpu.VMEM((SEQ, SITES, WIDTH), BF16),
            pltpu.VMEM((2, SEQ * SITES, 128), F32),
            pltpu.VMEM((SEQ * SITES, WIDTH), BF16),
            pltpu.VMEM((4, BLOCK, 128), F32),
            pltpu.VMEM((16, SLOT, SEQ), BF16),
            pltpu.VMEM((8, SLOT, SEQ), BF16),
            pltpu.VMEM((4, 64, SEQ), BF16),
            pltpu.VMEM((SEQ, 2048), BF16),
            pltpu.VMEM((SEQ, 128), BF16),
            pltpu.VMEM((PROJ * PROJ, PAIR), F32),
            pltpu.VMEM((2 * PAIR, 512), BF16),
            pltpu.VMEM((SITES, 512, 128), BF16),
            pltpu.VMEM((8192, PAIR), BF16),
            pltpu.SemaphoreType.DMA((10,)),
            pltpu.SemaphoreType.DMA((NCHUNK,)),
            pltpu.SemaphoreType.DMA((16,)),
            pltpu.SemaphoreType.DMA((16,)),
            pltpu.SemaphoreType.DMA,
            pltpu.SemaphoreType.DMA((8,)),
            pltpu.SemaphoreType.DMA((8,)),
            pltpu.SemaphoreType.DMA,
            pltpu.SemaphoreType.DMA,
            pltpu.SemaphoreType.DMA,
            pltpu.SemaphoreType.DMA,
            pltpu.SemaphoreType.REGULAR,
        ],
        compiler_params=pltpu.CompilerParams(
            collective_id=0, has_side_effects=True, vmem_limit_bytes=60 << 20
        ),
    )(
        x, marks, gain1[None], shift1[None], wl.T, bl[None], wr.T, br[None], wd, gain2[None], shift2[None]
    )
    pair = pair.reshape(128, 8, 8, PAIR)
    rows = rows.reshape(NDEV, 4, SITES, WIDTH).transpose(1, 0, 2, 3).reshape(4, 1024, WIDTH)
    return pair, rows


def solution(mesh):
    everywhere = P()
    return jax.shard_map(
        body,
        mesh=mesh,
        in_specs=(P(None, ("grp", "dev"), None), P(("grp", "dev"), None)) + (everywhere,) * 9,
        out_specs=(P("grp", None, "dev", None), P(("grp", "dev"), None, None)),
        check_vma=False,
    )
```

```python
import jax
import jax.numpy as jnp
from jax import lax
from jax.experimental import pallas as pl
from jax.experimental.pallas import tpu as pltpu
from jax.sharding import PartitionSpec as P

MESH = pl.DeviceIdType.MESH
F32 = jnp.float32
BF16 = jnp.bfloat16

SEQ = 512
SITES = 8
WIDTH = 256
PROJ = 32
PAIR = 128
NDEV = 128
CHUNK = 128
NCHUNK = SEQ // CHUNK
BLOCK = SITES * PROJ
SLOT = BLOCK + 16
HALF = 128
EARLY, PER = 4, 2


def place():
    g = lax.axis_index("grp")
    d = lax.axis_index("dev")
    return g, d


def coords(g, d):
    return (d // 2 % 2) * 2 + g % 2, d // 4, g // 2, d % 2


def remote(src, dst, send, recv, target):
    return pltpu.make_async_remote_copy(
        src_ref=src, dst_ref=dst, send_sem=send, recv_sem=recv, device_id=target, device_id_type=MESH
    )


def column(row):
    n = row.shape[1]
    a = lax.broadcasted_iota(jnp.int32, (n, n), 0)
    b = lax.broadcasted_iota(jnp.int32, (n, n), 1)
    return jnp.sum(jnp.where(a == b, jnp.broadcast_to(row, (n, n)), 0.0), axis=1, keepdims=True)


def kernel(
    x_hbm, marks_h, gain1_h, shift1_h, wl_h, bl_h, wr_h, br_h, wd_h, gain2_h, shift2_h,
    pair_out, row_hbm,
    marks, gain1, shift1, wl, bl, wr, br, wd, gain2, shift2,
    xv, nf, rowbuf, rf, lslot, rslot, ra, rt, mrt, wf, w2, xs,
    psem, xsem, lrecv, lrecv2, lsend, rrecv, rrecv2, rsend, asend, arecv,
):
    g, d = place()
    me = g * 16 + d
    x0, y0, z0, c0 = coords(g, d)
    xh0 = d // 2 % 2

    groups = [
        (z0 + dz) % 4 * 2 + (g + dx) % 2 for dx, dz in
        ((0, 1), (1, 3), (0, 3), (1, 1), (0, 2), (1, 2), (1, 0), (0, 0))
    ]

    def column_of(q):
        o = lax.rem(q, 4)
        u = lax.rem(lax.div(q, 4) + 1, 4)
        dy = 1 + 2 * o + lax.div(o, 2) * (5 - 4 * o)
        return (
            lax.rem(y0 + dy, 4) * 4
            + lax.rem(xh0 + lax.div(u, 2), 2) * 2
            + lax.rem(c0 + lax.rem(u, 2), 2)
        )

    def xcopy(k):
        return pltpu.make_async_copy(
            x_hbm.at[pl.ds(k * CHUNK, CHUNK)], xv.at[pl.ds(k * CHUNK, CHUNK)], xsem.at[k]
        )

    small = (
        (gain1_h, gain1), (shift1_h, shift1), (gain2_h, gain2), (shift2_h, shift2), (marks_h, marks),
        (wl_h, wl), (wr_h, wr), (bl_h, bl), (br_h, br), (wd_h, wd),
    )
    for k, (a, b) in enumerate(small):
        pltpu.make_async_copy(a, b, psem.at[k]).start()
    for k in range(NCHUNK):
        xcopy(k).start()

    barrier = pltpu.get_barrier_semaphore()
    columns = [column_of(q) for q in range(16)]
    for td in columns:
        for tg in groups[: 7 if td is columns[15] else 8]:
            pl.semaphore_signal(barrier, inc=1, device_id=(tg, td), device_id_type=MESH)

    for k, (a, b) in enumerate(small):
        pltpu.make_async_copy(a, b, psem.at[k]).wait()

    def norm(k, carry):
        xcopy(k).wait()
        x = xv[pl.ds(k * CHUNK, CHUNK)].astype(F32).reshape(CHUNK * SITES, WIDTH)
        mean = jnp.sum(x, axis=-1, keepdims=True) * (1.0 / WIDTH)
        cen = x - mean
        var = jnp.sum(cen * cen, axis=-1, keepdims=True) * (1.0 / WIDTH)
        scaled = cen * lax.rsqrt(var + 1e-05)
        rows = pl.ds(pl.multiple_of(k * CHUNK * SITES, CHUNK * SITES), CHUNK * SITES)
        rowbuf[rows, :] = (scaled * gain2[...] + shift2[...]).astype(BF16)
        normed = scaled * gain1[...] + shift1[...]
        nf[0, rows, :] = normed[:, :128]
        nf[1, rows, :] = normed[:, 128:]
        return carry

    lax.fori_loop(0, NCHUNK, norm, 0)

    pl.semaphore_wait(barrier, NDEV - 1)

    def send_rows(q, targets):
        td = column_of(q)
        for tg in targets:
            to = tg * 16 + td
            remote(
                rowbuf.at[pl.ds(pl.multiple_of(to * 32, 32), 32)],
                row_hbm.at[pl.ds(pl.multiple_of(me * 32, 32), 32)],
                asend, arecv, (tg, td),
            ).start()

    def send_level(q, carry):
        send_rows(q, groups[6:])
        return carry

    def send_across(q, carry):
        send_rows(q, groups[:6])
        return carry

    mine = pl.ds(pl.multiple_of(me * 32, 32), 32)
    pltpu.make_async_copy(rowbuf.at[mine], row_hbm.at[mine], arecv).start()

    wt = jnp.concatenate([wl[...], wr[...]], axis=0)
    bias = jnp.concatenate([column(bl[...]), column(br[...])], axis=0)
    mask = marks[...].astype(F32)
    mask16 = jnp.concatenate([mask, jnp.zeros_like(mask)], axis=0).astype(BF16)
    for i in range(SITES):
        rows = jnp.concatenate(
            [nf[0, pl.ds(i, SEQ, stride=SITES), :], nf[1, pl.ds(i, SEQ, stride=SITES), :]], axis=1
        ).astype(BF16)
        p = lax.dot_general(wt, rows, (((1,), (1,)), ((), ())), preferred_element_type=F32)
        p = (p + bias) * mask[i : i + 1, :]
        lslot[d, pl.ds(i * PROJ, PROJ), :] = p[:PROJ].astype(BF16)
        for h in range(4):
            rf[h, pl.ds(i, PROJ, stride=SITES), :] = p[PROJ:, h * 128 : (h + 1) * 128]
    for h in range(4):
        rslot[g, pl.ds(0, BLOCK), pl.ds(h * 128, 128)] = rf[h].astype(BF16)
    lslot[d, pl.ds(BLOCK, 16), :] = mask16
    rslot[g, pl.ds(BLOCK, 16), :] = mask16

    def left_slot(dy, dxh, dc):
        return lax.rem(y0 + dy, 4) * 4 + lax.rem(xh0 + dxh, 2) * 2 + lax.rem(c0 + dc, 2)

    def right_slot(dz, dxl):
        return lax.rem(z0 + dz, 4) * 2 + lax.rem(g + dxl, 2)

    halves = (pl.ds(0, HALF), pl.ds(HALF, SLOT - HALF))
    lsems, rsems = (lrecv, lrecv2), (rrecv, rrecv2)
    here = (g, d)

    def left(slot, h, target):
        at = lslot.at[slot, halves[h]]
        return remote(at, at, lsend, lsems[h].at[slot], target)

    def right(slot, h, target):
        at = rslot.at[slot, halves[h]]
        return remote(at, at, rsend, rsems[h].at[slot], target)

    def whole(slot, target):
        return remote(lslot.at[slot], lslot.at[slot], lsend, lrecv.at[slot], target)

    sibling = (g, left_slot(0, 0, 1))
    lpartner = left_slot(0, 1, 0)
    rpartner = right_slot(0, 1)
    lup, ldown = (g, left_slot(1, 0, 0)), (g, left_slot(3, 0, 0))
    rup, rdown = (right_slot(1, 0), d), (right_slot(3, 0), d)

    def both_ways(send, slot, up, down):
        send(slot, 0, up).start()
        send(slot, 1, down).start()
        send(slot, 1, up).start()
        send(slot, 0, down).start()

    def onward(send, low, high, up, down):
        send(low, 0, here).wait_recv()
        send(low, 0, up).start()
        send(high, 1, here).wait_recv()
        send(high, 1, down).start()

    def share(k):
        low, high = left_slot(3, k, 0), left_slot(1, k, 0)
        left(low, 1, here).wait_recv()
        whole(low, sibling).start()
        left(high, 0, here).wait_recv()
        whole(high, sibling).start()

    def share_far(k):
        far = left_slot(2, k, 0)
        left(far, 0, here).wait_recv()
        left(far, 1, here).wait_recv()
        whole(far, sibling).start()

    right(g, 0, (rpartner, d)).start()
    right(g, 1, (rpartner, d)).start()
    both_ways(right, g, rup, rdown)
    both_ways(left, d, lup, ldown)
    whole(d, sibling).start()

    lax.fori_loop(0, 15, send_level, 0)
    send_rows(15, groups[6:7])

    right(rpartner, 0, here).wait_recv()
    right(rpartner, 0, rup).start()
    right(rpartner, 0, rdown).start()
    left(d, 0, (g, lpartner)).start()
    left(d, 1, (g, lpartner)).start()
    right(rpartner, 1, here).wait_recv()
    right(rpartner, 1, rdown).start()
    right(rpartner, 1, rup).start()
    onward(right, right_slot(3, 0), right_slot(1, 0), rup, rdown)
    onward(left, left_slot(3, 0, 0), left_slot(1, 0, 0), lup, ldown)
    share(0)
    onward(right, right_slot(3, 1), right_slot(1, 1), rup, rdown)
    left(lpartner, 0, here).wait_recv()
    left(lpartner, 0, lup).start()
    left(lpartner, 0, ldown).start()
    left(lpartner, 1, here).wait_recv()
    left(lpartner, 1, ldown).start()
    left(lpartner, 1, lup).start()
    whole(lpartner, sibling).start()
    lax.fori_loop(0, EARLY, send_across, 0)
    share_far(0)

    wf[...] = wd[...].astype(F32)
    for e2 in range(2):
        stack = jnp.concatenate(
            [wf[pl.ds(2 * ep + e2, PROJ, stride=PROJ), :] for ep in range(PROJ // 2)], axis=0
        )
        w2[pl.ds(e2 * PAIR, PAIR), :] = stack.T.astype(BF16)

    for k in range(2):
        right(right_slot(3, k), 1, here).wait_recv()
        right(right_slot(1, k), 0, here).wait_recv()
        right(right_slot(2, k), 0, here).wait_recv()
        right(right_slot(2, k), 1, here).wait_recv()

    def merge(t, carry):
        e = pl.multiple_of(t * 4 * SITES, 4 * SITES)
        for q in range(4):
            a = rslot[2 * q, pl.ds(e, 4 * SITES), :].astype(F32).reshape(4, SITES, SEQ)
            b = rslot[2 * q + 1, pl.ds(e, 4 * SITES), :].astype(F32).reshape(4, SITES, SEQ)
            ra[:, pl.ds(q * 16, 16), :] = jnp.concatenate([a, b], axis=1).astype(BF16)
        for h in range(2):
            block = ra[2 * h : 2 * h + 2].reshape(128, SEQ)
            lanes = pl.ds(pl.multiple_of(t * 256 + h * 128, 128), 128)
            rt[:, lanes] = block.T
        return carry

    lax.fori_loop(0, PROJ // 4, merge, 0)
    mr = jnp.concatenate(
        [rslot[k, pl.ds(BLOCK, 16), :].astype(F32)[:SITES] for k in range(8)], axis=0
    )
    mrt[...] = jnp.concatenate([mr, mr], axis=0).astype(BF16).T

    low = lax.broadcasted_iota(jnp.int32, (1, 128), 1) < 64

    def outer(pair, buf):
        lhs = lslot[pl.ds(2 * pair, 2), pl.ds(0, BLOCK), :].reshape(2 * BLOCK, SEQ)
        for nb in range(8):
            x = jnp.dot(lhs, rt[:, nb * 256 : (nb + 1) * 256], preferred_element_type=F32).astype(BF16)
            for h in range(2):
                ep = nb * 2 + h
                for i in range(2 * SITES):
                    xs[buf, i, ep * PROJ : (ep + 1) * PROJ, :] = x[
                        i * PROJ : (i + 1) * PROJ, h * 128 : (h + 1) * 128
                    ]

    def combine(pair, buf):
        marks2 = lslot[pl.ds(2 * pair, 2), pl.ds(BLOCK, 16), :].reshape(32, SEQ)
        count = jnp.dot(marks2, mrt[...], preferred_element_type=F32)
        inverse = 1.0 / (count + 0.001)
        for i in range(0, 2 * SITES, 2):
            rhs = jnp.concatenate([xs[buf, i], xs[buf, i + 1]], axis=1)
            y = jnp.dot(w2[...], rhs, preferred_element_type=F32)
            a, b = y[:PAIR], y[PAIR:]
            early = a[:, :128] + pltpu.roll(b[:, :128], 64, axis=1)
            late = b[:, 128:] + pltpu.roll(a[:, 128:], 64, axis=1)
            both = jnp.where(low, early, late)
            m = i // SITES * 16 + i % SITES
            scale = jnp.where(low, inverse[m : m + 1], inverse[m + 1 : m + 2])
            at = pl.ds(pl.multiple_of(pair * 1024 + i * 64, 128), 128)
            pair_out[at, :] = (both * scale).astype(BF16).T

    def pair_at(t):
        o = lax.rem(t, 4)
        dy = o + lax.div(o, 2) * (5 - 2 * o)
        return lax.rem(y0 + dy, 4) * 2 + lax.rem(xh0 + lax.div(t, 4), 2)

    def await_sibling(t):
        whole(2 * pair_at(t) + 1 - c0, here).wait_recv()

    def step(t, carry):
        @pl.when(t == 1)
        def _():
            onward(left, left_slot(3, 1, 0), left_slot(1, 1, 0), lup, ldown)

        @pl.when(t == 2)
        def _():
            share(1)

        @pl.when(t == 3)
        def _():
            share_far(1)

        for k in range(PER):
            q = EARLY + (t - 1) * PER + k

            @pl.when(q < 16)
            def _():
                send_across(q, 0)

        await_sibling(t)
        now = lax.rem(t, 2)
        combine(pair_at(t - 1), 1 - now)
        outer(pair_at(t), now)
        return carry

    await_sibling(0)
    outer(pair_at(0), 0)
    lax.fori_loop(1, 8, step, 0)
    combine(pair_at(7), 1)

    pltpu.make_async_copy(lslot.at[pl.ds(0, 15)], lslot.at[pl.ds(0, 15)], lsend).wait()
    pltpu.make_async_copy(rslot.at[pl.ds(0, 7)], rslot.at[pl.ds(0, 7)], rsend).wait()
    rest = pl.ds(0, (NDEV - 1) * 32)
    pltpu.make_async_copy(rowbuf.at[rest], rowbuf.at[rest], asend).wait()
    pltpu.make_async_copy(rowbuf, row_hbm, arecv).wait()


def body(x, marks, gain1, shift1, wl, bl, wr, br, wd, gain2, shift2):
    hbm = pl.BlockSpec(memory_space=pltpu.HBM)
    free = pl.BlockSpec(memory_space=pl.ANY)
    pair, rows = pl.pallas_call(
        kernel,
        out_shape=(
            jax.ShapeDtypeStruct((8192, PAIR), BF16),
            jax.ShapeDtypeStruct((NDEV * 32, WIDTH), BF16),
        ),
        in_specs=[hbm] * 11,
        out_specs=(pl.BlockSpec(memory_space=pltpu.VMEM), free),
        scratch_shapes=[
            pltpu.VMEM((SITES, SEQ), jnp.int32),
            pltpu.VMEM((1, WIDTH), F32),
            pltpu.VMEM((1, WIDTH), F32),
            pltpu.VMEM((PROJ, WIDTH), BF16),
            pltpu.VMEM((1, PROJ), F32),
            pltpu.VMEM((PROJ, WIDTH), BF16),
            pltpu.VMEM((1, PROJ), F32),
            pltpu.VMEM((PROJ * PROJ, PAIR), BF16),
            pltpu.VMEM((1, WIDTH), F32),
            pltpu.VMEM((1, WIDTH), F32),
            pltpu.VMEM((SEQ, SITES, WIDTH), BF16),
            pltpu.VMEM((2, SEQ * SITES, 128), F32),
            pltpu.VMEM((SEQ * SITES, WIDTH), BF16),
            pltpu.VMEM((4, BLOCK, 128), F32),
            pltpu.VMEM((16, SLOT, SEQ), BF16),
            pltpu.VMEM((8, SLOT, SEQ), BF16),
            pltpu.VMEM((4, 64, SEQ), BF16),
            pltpu.VMEM((SEQ, 2048), BF16),
            pltpu.VMEM((SEQ, 128), BF16),
            pltpu.VMEM((PROJ * PROJ, PAIR), F32),
            pltpu.VMEM((2 * PAIR, 512), BF16),
            pltpu.VMEM((2, 2 * SITES, 512, 128), BF16),
            pltpu.SemaphoreType.DMA((10,)),
            pltpu.SemaphoreType.DMA((NCHUNK,)),
            pltpu.SemaphoreType.DMA((16,)),
            pltpu.SemaphoreType.DMA((16,)),
            pltpu.SemaphoreType.DMA,
            pltpu.SemaphoreType.DMA((8,)),
            pltpu.SemaphoreType.DMA((8,)),
            pltpu.SemaphoreType.DMA,
            pltpu.SemaphoreType.DMA,
            pltpu.SemaphoreType.DMA,
        ],
        compiler_params=pltpu.CompilerParams(
            collective_id=0, has_side_effects=True, vmem_limit_bytes=44 << 20
        ),
    )(
        *(
            pltpu.with_memory_space_constraint(v, pltpu.HBM)
            for v in (
                x, marks, gain1[None], shift1[None], wl.T, bl[None], wr.T, br[None], wd,
                gain2[None], shift2[None],
            )
        )
    )
    pair = pair.reshape(128, 8, 8, PAIR)
    rows = rows.reshape(NDEV, 4, SITES, WIDTH).transpose(1, 0, 2, 3).reshape(4, 1024, WIDTH)
    return pair, rows


def solution(mesh):
    everywhere = P()
    return jax.shard_map(
        body,
        mesh=mesh,
        in_specs=(P(None, ("grp", "dev"), None), P(("grp", "dev"), None)) + (everywhere,) * 9,
        out_specs=(P("grp", None, "dev", None), P(("grp", "dev"), None, None)),
        check_vma=False,
    )
```

```python
import jax
import jax.numpy as jnp
from jax import lax
from jax.experimental import pallas as pl
from jax.experimental.pallas import tpu as pltpu
from jax.sharding import PartitionSpec as P

MESH = pl.DeviceIdType.MESH
F32 = jnp.float32
BF16 = jnp.bfloat16

SEQ = 512
SITES = 8
WIDTH = 256
PROJ = 32
PAIR = 128
NDEV = 128
CHUNK = 128
NCHUNK = SEQ // CHUNK
BLOCK = SITES * PROJ
SLOT = BLOCK + 16
HALF = 128
EARLY, PER = 4, 2


def place():
    g = lax.axis_index("grp")
    d = lax.axis_index("dev")
    return g, d


def coords(g, d):
    return (d // 2 % 2) * 2 + g % 2, d // 4, g // 2, d % 2


def remote(src, dst, send, recv, target):
    return pltpu.make_async_remote_copy(
        src_ref=src, dst_ref=dst, send_sem=send, recv_sem=recv, device_id=target, device_id_type=MESH
    )


def column(row):
    n = row.shape[1]
    a = lax.broadcasted_iota(jnp.int32, (n, n), 0)
    b = lax.broadcasted_iota(jnp.int32, (n, n), 1)
    return jnp.sum(jnp.where(a == b, jnp.broadcast_to(row, (n, n)), 0.0), axis=1, keepdims=True)


def kernel(
    x_hbm, marks_h, gain1_h, shift1_h, wl_h, bl_h, wr_h, br_h, wd_h, gain2_h, shift2_h,
    pair_out, row_hbm,
    marks, gain1, shift1, wl, bl, wr, br, wd, gain2, shift2,
    xv, nf, rowbuf, rf, lslot, rslot, ra, rt, mrt, wf, w2, xs,
    psem, xsem, lrecv, lrecv2, lsend, rrecv, rrecv2, rsend, asend, arecv, plane, cube,
):
    g, d = place()
    me = g * 16 + d
    x0, y0, z0, c0 = coords(g, d)
    xh0 = d // 2 % 2

    groups = [
        (z0 + dz) % 4 * 2 + (g + dx) % 2 for dx, dz in
        ((0, 1), (1, 3), (0, 3), (1, 1), (0, 2), (1, 2), (1, 0), (0, 0))
    ]

    def column_of(q):
        o = lax.rem(q, 4)
        u = lax.rem(lax.div(q, 4) + 1, 4)
        dy = 1 + 2 * o + lax.div(o, 2) * (5 - 4 * o)
        return (
            lax.rem(y0 + dy, 4) * 4
            + lax.rem(xh0 + lax.div(u, 2), 2) * 2
            + lax.rem(c0 + lax.rem(u, 2), 2)
        )

    def xcopy(k):
        return pltpu.make_async_copy(
            x_hbm.at[pl.ds(k * CHUNK, CHUNK)], xv.at[pl.ds(k * CHUNK, CHUNK)], xsem.at[k]
        )

    small = (
        (gain1_h, gain1), (shift1_h, shift1), (gain2_h, gain2), (shift2_h, shift2), (marks_h, marks),
        (wl_h, wl), (wr_h, wr), (bl_h, bl), (br_h, br), (wd_h, wd),
    )
    for k, (a, b) in enumerate(small):
        pltpu.make_async_copy(a, b, psem.at[k]).start()
    for k in range(NCHUNK):
        xcopy(k).start()

    def left_slot(dy, dxh, dc):
        return lax.rem(y0 + dy, 4) * 4 + lax.rem(xh0 + dxh, 2) * 2 + lax.rem(c0 + dc, 2)

    def right_slot(dz, dxl):
        return lax.rem(z0 + dz, 4) * 2 + lax.rem(g + dxl, 2)

    ring_y = [(g, left_slot(k, 0, 0)) for k in (1, 3, 2)]
    ring_z = [(right_slot(k, 0), d) for k in (1, 3, 2)]
    row_x = [
        (right_slot(0, k // 4), left_slot(0, k // 2 % 2, k % 2)) for k in range(1, 8)
    ]
    barrier = pltpu.get_barrier_semaphore()
    for to in row_x + ring_y + ring_z:
        pl.semaphore_signal(barrier, inc=1, device_id=to, device_id_type=MESH)

    for k, (a, b) in enumerate(small):
        pltpu.make_async_copy(a, b, psem.at[k]).wait()

    def norm(k, carry):
        xcopy(k).wait()
        x = xv[pl.ds(k * CHUNK, CHUNK)].astype(F32).reshape(CHUNK * SITES, WIDTH)
        mean = jnp.sum(x, axis=-1, keepdims=True) * (1.0 / WIDTH)
        cen = x - mean
        var = jnp.sum(cen * cen, axis=-1, keepdims=True) * (1.0 / WIDTH)
        scaled = cen * lax.rsqrt(var + 1e-05)
        rows = pl.ds(pl.multiple_of(k * CHUNK * SITES, CHUNK * SITES), CHUNK * SITES)
        rowbuf[rows, :] = (scaled * gain2[...] + shift2[...]).astype(BF16)
        normed = scaled * gain1[...] + shift1[...]
        nf[0, rows, :] = normed[:, :128]
        nf[1, rows, :] = normed[:, 128:]
        return carry

    lax.fori_loop(0, NCHUNK, norm, 0)

    pl.semaphore_wait(barrier, 13)
    for to in ring_y:
        pl.semaphore_signal(plane, inc=1, device_id=to, device_id_type=MESH)

    def send_rows(q, targets):
        td = column_of(q)
        for tg in targets:
            to = tg * 16 + td
            remote(
                rowbuf.at[pl.ds(pl.multiple_of(to * 32, 32), 32)],
                row_hbm.at[pl.ds(pl.multiple_of(me * 32, 32), 32)],
                asend, arecv, (tg, td),
            ).start()

    def send_level(q, carry):
        send_rows(q, groups[6:])
        return carry

    def send_across(q, carry):
        send_rows(q, groups[:6])
        return carry

    mine = pl.ds(pl.multiple_of(me * 32, 32), 32)
    pltpu.make_async_copy(rowbuf.at[mine], row_hbm.at[mine], arecv).start()

    wt = jnp.concatenate([wl[...], wr[...]], axis=0)
    bias = jnp.concatenate([column(bl[...]), column(br[...])], axis=0)
    mask = marks[...].astype(F32)
    mask16 = jnp.concatenate([mask, jnp.zeros_like(mask)], axis=0).astype(BF16)
    for i in range(SITES):
        rows = jnp.concatenate(
            [nf[0, pl.ds(i, SEQ, stride=SITES), :], nf[1, pl.ds(i, SEQ, stride=SITES), :]], axis=1
        ).astype(BF16)
        p = lax.dot_general(wt, rows, (((1,), (1,)), ((), ())), preferred_element_type=F32)
        p = (p + bias) * mask[i : i + 1, :]
        lslot[d, pl.ds(i * PROJ, PROJ), :] = p[:PROJ].astype(BF16)
        for h in range(4):
            rf[h, pl.ds(i, PROJ, stride=SITES), :] = p[PROJ:, h * 128 : (h + 1) * 128]
    for h in range(4):
        rslot[g, pl.ds(0, BLOCK), pl.ds(h * 128, 128)] = rf[h].astype(BF16)
    lslot[d, pl.ds(BLOCK, 16), :] = mask16
    rslot[g, pl.ds(BLOCK, 16), :] = mask16

    halves = (pl.ds(0, HALF), pl.ds(HALF, SLOT - HALF))
    lsems, rsems = (lrecv, lrecv2), (rrecv, rrecv2)
    here = (g, d)

    def left(slot, h, target):
        at = lslot.at[slot, halves[h]]
        return remote(at, at, lsend, lsems[h].at[slot], target)

    def right(slot, h, target):
        at = rslot.at[slot, halves[h]]
        return remote(at, at, rsend, rsems[h].at[slot], target)

    def whole(slot, target):
        return remote(lslot.at[slot], lslot.at[slot], lsend, lrecv.at[slot], target)

    sibling = (g, left_slot(0, 0, 1))
    lpartner = left_slot(0, 1, 0)
    rpartner = right_slot(0, 1)
    lup, ldown = (g, left_slot(1, 0, 0)), (g, left_slot(3, 0, 0))
    rup, rdown = (right_slot(1, 0), d), (right_slot(3, 0), d)

    def both_ways(send, slot, up, down):
        send(slot, 0, up).start()
        send(slot, 1, down).start()
        send(slot, 1, up).start()
        send(slot, 0, down).start()

    def onward(send, low, high, up, down):
        send(low, 0, here).wait_recv()
        send(low, 0, up).start()
        send(high, 1, here).wait_recv()
        send(high, 1, down).start()

    def share(k):
        low, high = left_slot(3, k, 0), left_slot(1, k, 0)
        left(low, 1, here).wait_recv()
        whole(low, sibling).start()
        left(high, 0, here).wait_recv()
        whole(high, sibling).start()

    def share_far(k):
        far = left_slot(2, k, 0)
        left(far, 0, here).wait_recv()
        left(far, 1, here).wait_recv()
        whole(far, sibling).start()

    right(g, 0, (rpartner, d)).start()
    right(g, 1, (rpartner, d)).start()
    both_ways(right, g, rup, rdown)
    both_ways(left, d, lup, ldown)
    whole(d, sibling).start()

    pl.semaphore_wait(plane, 3)
    for to in ring_z:
        pl.semaphore_signal(cube, inc=1, device_id=to, device_id_type=MESH)
    lax.fori_loop(0, 15, send_level, 0)
    send_rows(15, groups[6:7])

    right(rpartner, 0, here).wait_recv()
    right(rpartner, 0, rup).start()
    right(rpartner, 0, rdown).start()
    left(d, 0, (g, lpartner)).start()
    left(d, 1, (g, lpartner)).start()
    right(rpartner, 1, here).wait_recv()
    right(rpartner, 1, rdown).start()
    right(rpartner, 1, rup).start()
    onward(right, right_slot(3, 0), right_slot(1, 0), rup, rdown)
    onward(left, left_slot(3, 0, 0), left_slot(1, 0, 0), lup, ldown)
    share(0)
    onward(right, right_slot(3, 1), right_slot(1, 1), rup, rdown)
    left(lpartner, 0, here).wait_recv()
    left(lpartner, 0, lup).start()
    left(lpartner, 0, ldown).start()
    left(lpartner, 1, here).wait_recv()
    left(lpartner, 1, ldown).start()
    left(lpartner, 1, lup).start()
    whole(lpartner, sibling).start()
    pl.semaphore_wait(cube, 3)
    lax.fori_loop(0, EARLY, send_across, 0)
    share_far(0)

    wf[...] = wd[...].astype(F32)
    for e2 in range(2):
        stack = jnp.concatenate(
            [wf[pl.ds(2 * ep + e2, PROJ, stride=PROJ), :] for ep in range(PROJ // 2)], axis=0
        )
        w2[pl.ds(e2 * PAIR, PAIR), :] = stack.T.astype(BF16)

    for k in range(2):
        right(right_slot(3, k), 1, here).wait_recv()
        right(right_slot(1, k), 0, here).wait_recv()
        right(right_slot(2, k), 0, here).wait_recv()
        right(right_slot(2, k), 1, here).wait_recv()

    def merge(t, carry):
        e = pl.multiple_of(t * 4 * SITES, 4 * SITES)
        for q in range(4):
            a = rslot[2 * q, pl.ds(e, 4 * SITES), :].astype(F32).reshape(4, SITES, SEQ)
            b = rslot[2 * q + 1, pl.ds(e, 4 * SITES), :].astype(F32).reshape(4, SITES, SEQ)
            ra[:, pl.ds(q * 16, 16), :] = jnp.concatenate([a, b], axis=1).astype(BF16)
        for h in range(2):
            block = ra[2 * h : 2 * h + 2].reshape(128, SEQ)
            lanes = pl.ds(pl.multiple_of(t * 256 + h * 128, 128), 128)
            rt[:, lanes] = block.T
        return carry

    lax.fori_loop(0, PROJ // 4, merge, 0)
    mr = jnp.concatenate(
        [rslot[k, pl.ds(BLOCK, 16), :].astype(F32)[:SITES] for k in range(8)], axis=0
    )
    mrt[...] = jnp.concatenate([mr, mr], axis=0).astype(BF16).T

    low = lax.broadcasted_iota(jnp.int32, (1, 128), 1) < 64

    def outer(pair, buf):
        lhs = lslot[pl.ds(2 * pair, 2), pl.ds(0, BLOCK), :].reshape(2 * BLOCK, SEQ)
        for nb in range(8):
            x = jnp.dot(lhs, rt[:, nb * 256 : (nb + 1) * 256], preferred_element_type=F32).astype(BF16)
            for h in range(2):
                ep = nb * 2 + h
                for i in range(2 * SITES):
                    xs[buf, i, ep * PROJ : (ep + 1) * PROJ, :] = x[
                        i * PROJ : (i + 1) * PROJ, h * 128 : (h + 1) * 128
                    ]

    def combine(pair, buf):
        marks2 = lslot[pl.ds(2 * pair, 2), pl.ds(BLOCK, 16), :].reshape(32, SEQ)
        count = jnp.dot(marks2, mrt[...], preferred_element_type=F32)
        inverse = 1.0 / (count + 0.001)
        for i in range(0, 2 * SITES, 2):
            rhs = jnp.concatenate([xs[buf, i], xs[buf, i + 1]], axis=1)
            y = jnp.dot(w2[...], rhs, preferred_element_type=F32)
            a, b = y[:PAIR], y[PAIR:]
            early = a[:, :128] + pltpu.roll(b[:, :128], 64, axis=1)
            late = b[:, 128:] + pltpu.roll(a[:, 128:], 64, axis=1)
            both = jnp.where(low, early, late)
            m = i // SITES * 16 + i % SITES
            scale = jnp.where(low, inverse[m : m + 1], inverse[m + 1 : m + 2])
            at = pl.ds(pl.multiple_of(pair * 1024 + i * 64, 128), 128)
            pair_out[at, :] = (both * scale).astype(BF16).T

    def pair_at(t):
        o = lax.rem(t, 4)
        dy = o + lax.div(o, 2) * (5 - 2 * o)
        return lax.rem(y0 + dy, 4) * 2 + lax.rem(xh0 + lax.div(t, 4), 2)

    def await_sibling(t):
        whole(2 * pair_at(t) + 1 - c0, here).wait_recv()

    def step(t, carry):
        @pl.when(t == 1)
        def _():
            onward(left, left_slot(3, 1, 0), left_slot(1, 1, 0), lup, ldown)

        @pl.when(t == 2)
        def _():
            share(1)

        @pl.when(t == 3)
        def _():
            share_far(1)

        for k in range(PER):
            q = EARLY + (t - 1) * PER + k

            @pl.when(q < 16)
            def _():
                send_across(q, 0)

        await_sibling(t)
        now = lax.rem(t, 2)
        combine(pair_at(t - 1), 1 - now)
        outer(pair_at(t), now)
        return carry

    await_sibling(0)
    outer(pair_at(0), 0)
    lax.fori_loop(1, 8, step, 0)
    combine(pair_at(7), 1)

    pltpu.make_async_copy(lslot.at[pl.ds(0, 15)], lslot.at[pl.ds(0, 15)], lsend).wait()
    pltpu.make_async_copy(rslot.at[pl.ds(0, 7)], rslot.at[pl.ds(0, 7)], rsend).wait()
    rest = pl.ds(0, (NDEV - 1) * 32)
    pltpu.make_async_copy(rowbuf.at[rest], rowbuf.at[rest], asend).wait()
    pltpu.make_async_copy(rowbuf, row_hbm, arecv).wait()


def body(x, marks, gain1, shift1, wl, bl, wr, br, wd, gain2, shift2):
    hbm = pl.BlockSpec(memory_space=pltpu.HBM)
    free = pl.BlockSpec(memory_space=pl.ANY)
    pair, rows = pl.pallas_call(
        kernel,
        out_shape=(
            jax.ShapeDtypeStruct((8192, PAIR), BF16),
            jax.ShapeDtypeStruct((NDEV * 32, WIDTH), BF16),
        ),
        in_specs=[hbm] * 11,
        out_specs=(pl.BlockSpec(memory_space=pltpu.VMEM), free),
        scratch_shapes=[
            pltpu.VMEM((SITES, SEQ), jnp.int32),
            pltpu.VMEM((1, WIDTH), F32),
            pltpu.VMEM((1, WIDTH), F32),
            pltpu.VMEM((PROJ, WIDTH), BF16),
            pltpu.VMEM((1, PROJ), F32),
            pltpu.VMEM((PROJ, WIDTH), BF16),
            pltpu.VMEM((1, PROJ), F32),
            pltpu.VMEM((PROJ * PROJ, PAIR), BF16),
            pltpu.VMEM((1, WIDTH), F32),
            pltpu.VMEM((1, WIDTH), F32),
            pltpu.VMEM((SEQ, SITES, WIDTH), BF16),
            pltpu.VMEM((2, SEQ * SITES, 128), F32),
            pltpu.VMEM((SEQ * SITES, WIDTH), BF16),
            pltpu.VMEM((4, BLOCK, 128), F32),
            pltpu.VMEM((16, SLOT, SEQ), BF16),
            pltpu.VMEM((8, SLOT, SEQ), BF16),
            pltpu.VMEM((4, 64, SEQ), BF16),
            pltpu.VMEM((SEQ, 2048), BF16),
            pltpu.VMEM((SEQ, 128), BF16),
            pltpu.VMEM((PROJ * PROJ, PAIR), F32),
            pltpu.VMEM((2 * PAIR, 512), BF16),
            pltpu.VMEM((2, 2 * SITES, 512, 128), BF16),
            pltpu.SemaphoreType.DMA((10,)),
            pltpu.SemaphoreType.DMA((NCHUNK,)),
            pltpu.SemaphoreType.DMA((16,)),
            pltpu.SemaphoreType.DMA((16,)),
            pltpu.SemaphoreType.DMA,
            pltpu.SemaphoreType.DMA((8,)),
            pltpu.SemaphoreType.DMA((8,)),
            pltpu.SemaphoreType.DMA,
            pltpu.SemaphoreType.DMA,
            pltpu.SemaphoreType.DMA,
            pltpu.SemaphoreType.REGULAR,
            pltpu.SemaphoreType.REGULAR,
        ],
        compiler_params=pltpu.CompilerParams(
            collective_id=0, has_side_effects=True, vmem_limit_bytes=44 << 20
        ),
    )(
        *(
            pltpu.with_memory_space_constraint(v, pltpu.HBM)
            for v in (
                x, marks, gain1[None], shift1[None], wl.T, bl[None], wr.T, br[None], wd,
                gain2[None], shift2[None],
            )
        )
    )
    pair = pair.reshape(128, 8, 8, PAIR)
    rows = rows.reshape(NDEV, 4, SITES, WIDTH).transpose(1, 0, 2, 3).reshape(4, 1024, WIDTH)
    return pair, rows


def solution(mesh):
    everywhere = P()
    return jax.shard_map(
        body,
        mesh=mesh,
        in_specs=(P(None, ("grp", "dev"), None), P(("grp", "dev"), None)) + (everywhere,) * 9,
        out_specs=(P("grp", None, "dev", None), P(("grp", "dev"), None, None)),
        check_vma=False,
    )
```

```python
import jax
import jax.numpy as jnp
from jax import lax
from jax.experimental import pallas as pl
from jax.experimental.pallas import tpu as pltpu
from jax.sharding import PartitionSpec as P

MESH = pl.DeviceIdType.MESH
F32 = jnp.float32
BF16 = jnp.bfloat16

SEQ = 512
SITES = 8
WIDTH = 256
PROJ = 32
PAIR = 128
NDEV = 128
CHUNK = 128
NCHUNK = SEQ // CHUNK
BLOCK = SITES * PROJ
SLOT = BLOCK + 16
HALF = 128
EARLY, PER = 4, 2


def place():
    g = lax.axis_index("grp")
    d = lax.axis_index("dev")
    return g, d


def coords(g, d):
    return (d // 2 % 2) * 2 + g % 2, d // 4, g // 2, d % 2


def remote(src, dst, send, recv, target):
    return pltpu.make_async_remote_copy(
        src_ref=src, dst_ref=dst, send_sem=send, recv_sem=recv, device_id=target, device_id_type=MESH
    )


def column(row):
    n = row.shape[1]
    a = lax.broadcasted_iota(jnp.int32, (n, n), 0)
    b = lax.broadcasted_iota(jnp.int32, (n, n), 1)
    return jnp.sum(jnp.where(a == b, jnp.broadcast_to(row, (n, n)), 0.0), axis=1, keepdims=True)


def kernel(
    x_hbm, marks_h, gain1_h, shift1_h, wl_h, bl_h, wr_h, br_h, wd_h, gain2_h, shift2_h,
    pair_out, row_hbm,
    marks, gain1, shift1, wl, bl, wr, br, wd, gain2, shift2,
    xv, nf, rowbuf, rf, lslot, rslot, ra, rt, mrt, wf, w2, xs,
    psem, xsem, lrecv, lrecv2, lsend, rrecv, rrecv2, rsend, asend, arecv, plane, cube,
):
    g, d = place()
    me = g * 16 + d
    x0, y0, z0, c0 = coords(g, d)
    xh0 = d // 2 % 2

    groups = [
        (z0 + dz) % 4 * 2 + (g + dx) % 2 for dx, dz in
        ((0, 1), (1, 3), (0, 3), (1, 1), (0, 2), (1, 2), (1, 0), (0, 0))
    ]

    def column_of(q):
        o = lax.rem(q, 4)
        u = lax.rem(lax.div(q, 4) + 1, 4)
        dy = 1 + 2 * o + lax.div(o, 2) * (5 - 4 * o)
        return (
            lax.rem(y0 + dy, 4) * 4
            + lax.rem(xh0 + lax.div(u, 2), 2) * 2
            + lax.rem(c0 + lax.rem(u, 2), 2)
        )

    def xcopy(k):
        return pltpu.make_async_copy(
            x_hbm.at[pl.ds(k * CHUNK, CHUNK)], xv.at[pl.ds(k * CHUNK, CHUNK)], xsem.at[k]
        )

    small = (
        (gain1_h, gain1), (shift1_h, shift1), (gain2_h, gain2), (shift2_h, shift2), (marks_h, marks),
        (wl_h, wl), (wr_h, wr), (bl_h, bl), (br_h, br), (wd_h, wd),
    )
    for k, (a, b) in enumerate(small):
        pltpu.make_async_copy(a, b, psem.at[k]).start()
    for k in range(NCHUNK):
        xcopy(k).start()

    def left_slot(dy, dxh, dc):
        return lax.rem(y0 + dy, 4) * 4 + lax.rem(xh0 + dxh, 2) * 2 + lax.rem(c0 + dc, 2)

    def right_slot(dz, dxl):
        return lax.rem(z0 + dz, 4) * 2 + lax.rem(g + dxl, 2)

    ring_y = [(g, left_slot(k, 0, 0)) for k in (1, 3, 2)]
    ring_z = [(right_slot(k, 0), d) for k in (1, 3, 2)]
    row_x = [
        (right_slot(0, k // 4), left_slot(0, k // 2 % 2, k % 2)) for k in range(1, 8)
    ]
    barrier = pltpu.get_barrier_semaphore()
    for to in row_x + ring_y + ring_z:
        pl.semaphore_signal(barrier, inc=1, device_id=to, device_id_type=MESH)

    for k, (a, b) in enumerate(small):
        pltpu.make_async_copy(a, b, psem.at[k]).wait()

    def norm(k, carry):
        xcopy(k).wait()
        x = xv[pl.ds(k * CHUNK, CHUNK)].astype(F32).reshape(CHUNK * SITES, WIDTH)
        mean = jnp.sum(x, axis=-1, keepdims=True) * (1.0 / WIDTH)
        cen = x - mean
        var = jnp.sum(cen * cen, axis=-1, keepdims=True) * (1.0 / WIDTH)
        scaled = cen * lax.rsqrt(var + 1e-05)
        rows = pl.ds(pl.multiple_of(k * CHUNK * SITES, CHUNK * SITES), CHUNK * SITES)
        rowbuf[rows, :] = (scaled * gain2[...] + shift2[...]).astype(BF16)
        normed = scaled * gain1[...] + shift1[...]
        nf[0, rows, :] = normed[:, :128]
        nf[1, rows, :] = normed[:, 128:]
        return carry

    lax.fori_loop(0, NCHUNK, norm, 0)

    pl.semaphore_wait(barrier, 13)
    for to in ring_y:
        pl.semaphore_signal(plane, inc=1, device_id=to, device_id_type=MESH)

    def send_rows(q, targets):
        td = column_of(q)
        for tg in targets:
            to = tg * 16 + td
            remote(
                rowbuf.at[pl.ds(pl.multiple_of(to * 32, 32), 32)],
                row_hbm.at[pl.ds(pl.multiple_of(me * 32, 32), 32)],
                asend, arecv, (tg, td),
            ).start()

    def send_level(q, carry):
        send_rows(q, groups[6:])
        return carry

    def send_across(q, carry):
        send_rows(q, groups[:6])
        return carry

    mine = pl.ds(pl.multiple_of(me * 32, 32), 32)
    pltpu.make_async_copy(rowbuf.at[mine], row_hbm.at[mine], arecv).start()

    wt = jnp.concatenate([wl[...], wr[...]], axis=0)
    bias = jnp.concatenate([column(bl[...]), column(br[...])], axis=0)
    mask = marks[...].astype(F32)
    mask16 = jnp.concatenate([mask, jnp.zeros_like(mask)], axis=0).astype(BF16)
    for i in range(SITES):
        rows = jnp.concatenate(
            [nf[0, pl.ds(i, SEQ, stride=SITES), :], nf[1, pl.ds(i, SEQ, stride=SITES), :]], axis=1
        ).astype(BF16)
        p = lax.dot_general(wt, rows, (((1,), (1,)), ((), ())), preferred_element_type=F32)
        p = (p + bias) * mask[i : i + 1, :]
        lslot[d, pl.ds(i * PROJ, PROJ), :] = p[:PROJ].astype(BF16)
        for h in range(4):
            rf[h, pl.ds(i, PROJ, stride=SITES), :] = p[PROJ:, h * 128 : (h + 1) * 128]
    for h in range(4):
        rslot[g, pl.ds(0, BLOCK), pl.ds(h * 128, 128)] = rf[h].astype(BF16)
    lslot[d, pl.ds(BLOCK, 16), :] = mask16
    rslot[g, pl.ds(BLOCK, 16), :] = mask16

    halves = (pl.ds(0, HALF), pl.ds(HALF, SLOT - HALF))
    lsems, rsems = (lrecv, lrecv2), (rrecv, rrecv2)
    here = (g, d)

    def left(slot, h, target):
        at = lslot.at[slot, halves[h]]
        return remote(at, at, lsend, lsems[h].at[slot], target)

    def right(slot, h, target):
        at = rslot.at[slot, halves[h]]
        return remote(at, at, rsend, rsems[h].at[slot], target)

    def whole(slot, target):
        return remote(lslot.at[slot], lslot.at[slot], lsend, lrecv.at[slot], target)

    sibling = (g, left_slot(0, 0, 1))
    lpartner = left_slot(0, 1, 0)
    rpartner = right_slot(0, 1)
    lup, ldown = (g, left_slot(1, 0, 0)), (g, left_slot(3, 0, 0))
    rup, rdown = (right_slot(1, 0), d), (right_slot(3, 0), d)

    def both_ways(send, slot, up, down):
        send(slot, 0, up).start()
        send(slot, 1, down).start()
        send(slot, 1, up).start()
        send(slot, 0, down).start()

    def onward(send, low, high, up, down):
        send(low, 0, here).wait_recv()
        send(low, 0, up).start()
        send(high, 1, here).wait_recv()
        send(high, 1, down).start()

    def share(k):
        low, high = left_slot(3, k, 0), left_slot(1, k, 0)
        left(low, 1, here).wait_recv()
        whole(low, sibling).start()
        left(high, 0, here).wait_recv()
        whole(high, sibling).start()

    def share_far(k):
        far = left_slot(2, k, 0)
        left(far, 0, here).wait_recv()
        left(far, 1, here).wait_recv()
        whole(far, sibling).start()

    right(g, 0, (rpartner, d)).start()
    right(g, 1, (rpartner, d)).start()
    both_ways(right, g, rup, rdown)
    both_ways(left, d, lup, ldown)
    whole(d, sibling).start()
    left(d, 0, (g, lpartner)).start()
    left(d, 1, (g, lpartner)).start()

    pl.semaphore_wait(plane, 3)
    for to in ring_z:
        pl.semaphore_signal(cube, inc=1, device_id=to, device_id_type=MESH)
    lax.fori_loop(0, 15, send_level, 0)
    send_rows(15, groups[6:7])

    right(rpartner, 0, here).wait_recv()
    right(rpartner, 0, rup).start()
    right(rpartner, 0, rdown).start()
    right(rpartner, 1, here).wait_recv()
    right(rpartner, 1, rdown).start()
    right(rpartner, 1, rup).start()
    onward(right, right_slot(3, 0), right_slot(1, 0), rup, rdown)
    onward(left, left_slot(3, 0, 0), left_slot(1, 0, 0), lup, ldown)
    share(0)
    onward(right, right_slot(3, 1), right_slot(1, 1), rup, rdown)
    left(lpartner, 0, here).wait_recv()
    left(lpartner, 0, lup).start()
    left(lpartner, 0, ldown).start()
    left(lpartner, 1, here).wait_recv()
    left(lpartner, 1, ldown).start()
    left(lpartner, 1, lup).start()
    whole(lpartner, sibling).start()
    pl.semaphore_wait(cube, 3)
    lax.fori_loop(0, EARLY, send_across, 0)
    share_far(0)

    wf[...] = wd[...].astype(F32)
    for e2 in range(2):
        stack = jnp.concatenate(
            [wf[pl.ds(2 * ep + e2, PROJ, stride=PROJ), :] for ep in range(PROJ // 2)], axis=0
        )
        w2[pl.ds(e2 * PAIR, PAIR), :] = stack.T.astype(BF16)

    for k in range(2):
        right(right_slot(3, k), 1, here).wait_recv()
        right(right_slot(1, k), 0, here).wait_recv()
        right(right_slot(2, k), 0, here).wait_recv()
        right(right_slot(2, k), 1, here).wait_recv()

    def merge(t, carry):
        e = pl.multiple_of(t * 4 * SITES, 4 * SITES)
        for q in range(4):
            a = rslot[2 * q, pl.ds(e, 4 * SITES), :].astype(F32).reshape(4, SITES, SEQ)
            b = rslot[2 * q + 1, pl.ds(e, 4 * SITES), :].astype(F32).reshape(4, SITES, SEQ)
            ra[:, pl.ds(q * 16, 16), :] = jnp.concatenate([a, b], axis=1).astype(BF16)
        for h in range(2):
            block = ra[2 * h : 2 * h + 2].reshape(128, SEQ)
            lanes = pl.ds(pl.multiple_of(t * 256 + h * 128, 128), 128)
            rt[:, lanes] = block.T
        return carry

    lax.fori_loop(0, PROJ // 4, merge, 0)
    mr = jnp.concatenate(
        [rslot[k, pl.ds(BLOCK, 16), :].astype(F32)[:SITES] for k in range(8)], axis=0
    )
    mrt[...] = jnp.concatenate([mr, mr], axis=0).astype(BF16).T

    low = lax.broadcasted_iota(jnp.int32, (1, 128), 1) < 64

    def outer(pair, buf):
        lhs = lslot[pl.ds(2 * pair, 2), pl.ds(0, BLOCK), :].reshape(2 * BLOCK, SEQ)
        for nb in range(8):
            x = jnp.dot(lhs, rt[:, nb * 256 : (nb + 1) * 256], preferred_element_type=F32).astype(BF16)
            for h in range(2):
                ep = nb * 2 + h
                for i in range(2 * SITES):
                    xs[buf, i, ep * PROJ : (ep + 1) * PROJ, :] = x[
                        i * PROJ : (i + 1) * PROJ, h * 128 : (h + 1) * 128
                    ]

    def combine(pair, buf):
        marks2 = lslot[pl.ds(2 * pair, 2), pl.ds(BLOCK, 16), :].reshape(32, SEQ)
        count = jnp.dot(marks2, mrt[...], preferred_element_type=F32)
        inverse = 1.0 / (count + 0.001)
        for i in range(0, 2 * SITES, 2):
            rhs = jnp.concatenate([xs[buf, i], xs[buf, i + 1]], axis=1)
            y = jnp.dot(w2[...], rhs, preferred_element_type=F32)
            a, b = y[:PAIR], y[PAIR:]
            early = a[:, :128] + pltpu.roll(b[:, :128], 64, axis=1)
            late = b[:, 128:] + pltpu.roll(a[:, 128:], 64, axis=1)
            both = jnp.where(low, early, late)
            m = i // SITES * 16 + i % SITES
            scale = jnp.where(low, inverse[m : m + 1], inverse[m + 1 : m + 2])
            at = pl.ds(pl.multiple_of(pair * 1024 + i * 64, 128), 128)
            pair_out[at, :] = (both * scale).astype(BF16).T

    def pair_at(t):
        o = lax.rem(t, 4)
        dy = o + lax.div(o, 2) * (5 - 2 * o)
        return lax.rem(y0 + dy, 4) * 2 + lax.rem(xh0 + lax.div(t, 4), 2)

    def await_sibling(t):
        whole(2 * pair_at(t) + 1 - c0, here).wait_recv()

    def step(t, carry):
        @pl.when(t == 1)
        def _():
            onward(left, left_slot(3, 1, 0), left_slot(1, 1, 0), lup, ldown)

        @pl.when(t == 2)
        def _():
            share(1)

        @pl.when(t == 3)
        def _():
            share_far(1)

        for k in range(PER):
            q = EARLY + (t - 1) * PER + k

            @pl.when(q < 16)
            def _():
                send_across(q, 0)

        await_sibling(t)
        now = lax.rem(t, 2)
        combine(pair_at(t - 1), 1 - now)
        outer(pair_at(t), now)
        return carry

    await_sibling(0)
    outer(pair_at(0), 0)
    lax.fori_loop(1, 8, step, 0)
    combine(pair_at(7), 1)

    pltpu.make_async_copy(lslot.at[pl.ds(0, 15)], lslot.at[pl.ds(0, 15)], lsend).wait()
    pltpu.make_async_copy(rslot.at[pl.ds(0, 7)], rslot.at[pl.ds(0, 7)], rsend).wait()
    rest = pl.ds(0, (NDEV - 1) * 32)
    pltpu.make_async_copy(rowbuf.at[rest], rowbuf.at[rest], asend).wait()
    pltpu.make_async_copy(rowbuf, row_hbm, arecv).wait()


def body(x, marks, gain1, shift1, wl, bl, wr, br, wd, gain2, shift2):
    hbm = pl.BlockSpec(memory_space=pltpu.HBM)
    free = pl.BlockSpec(memory_space=pl.ANY)
    pair, rows = pl.pallas_call(
        kernel,
        out_shape=(
            jax.ShapeDtypeStruct((8192, PAIR), BF16),
            jax.ShapeDtypeStruct((NDEV * 32, WIDTH), BF16),
        ),
        in_specs=[hbm] * 11,
        out_specs=(pl.BlockSpec(memory_space=pltpu.VMEM), free),
        scratch_shapes=[
            pltpu.VMEM((SITES, SEQ), jnp.int32),
            pltpu.VMEM((1, WIDTH), F32),
            pltpu.VMEM((1, WIDTH), F32),
            pltpu.VMEM((PROJ, WIDTH), BF16),
            pltpu.VMEM((1, PROJ), F32),
            pltpu.VMEM((PROJ, WIDTH), BF16),
            pltpu.VMEM((1, PROJ), F32),
            pltpu.VMEM((PROJ * PROJ, PAIR), BF16),
            pltpu.VMEM((1, WIDTH), F32),
            pltpu.VMEM((1, WIDTH), F32),
            pltpu.VMEM((SEQ, SITES, WIDTH), BF16),
            pltpu.VMEM((2, SEQ * SITES, 128), F32),
            pltpu.VMEM((SEQ * SITES, WIDTH), BF16),
            pltpu.VMEM((4, BLOCK, 128), F32),
            pltpu.VMEM((16, SLOT, SEQ), BF16),
            pltpu.VMEM((8, SLOT, SEQ), BF16),
            pltpu.VMEM((4, 64, SEQ), BF16),
            pltpu.VMEM((SEQ, 2048), BF16),
            pltpu.VMEM((SEQ, 128), BF16),
            pltpu.VMEM((PROJ * PROJ, PAIR), F32),
            pltpu.VMEM((2 * PAIR, 512), BF16),
            pltpu.VMEM((2, 2 * SITES, 512, 128), BF16),
            pltpu.SemaphoreType.DMA((10,)),
            pltpu.SemaphoreType.DMA((NCHUNK,)),
            pltpu.SemaphoreType.DMA((16,)),
            pltpu.SemaphoreType.DMA((16,)),
            pltpu.SemaphoreType.DMA,
            pltpu.SemaphoreType.DMA((8,)),
            pltpu.SemaphoreType.DMA((8,)),
            pltpu.SemaphoreType.DMA,
            pltpu.SemaphoreType.DMA,
            pltpu.SemaphoreType.DMA,
            pltpu.SemaphoreType.REGULAR,
            pltpu.SemaphoreType.REGULAR,
        ],
        compiler_params=pltpu.CompilerParams(
            collective_id=0, has_side_effects=True, vmem_limit_bytes=44 << 20
        ),
    )(
        *(
            pltpu.with_memory_space_constraint(v, pltpu.HBM)
            for v in (
                x, marks, gain1[None], shift1[None], wl.T, bl[None], wr.T, br[None], wd,
                gain2[None], shift2[None],
            )
        )
    )
    pair = pair.reshape(128, 8, 8, PAIR)
    rows = rows.reshape(NDEV, 4, SITES, WIDTH).transpose(1, 0, 2, 3).reshape(4, 1024, WIDTH)
    return pair, rows


def solution(mesh):
    everywhere = P()
    return jax.shard_map(
        body,
        mesh=mesh,
        in_specs=(P(None, ("grp", "dev"), None), P(("grp", "dev"), None)) + (everywhere,) * 9,
        out_specs=(P("grp", None, "dev", None), P(("grp", "dev"), None, None)),
        check_vma=False,
    )
```

```python
import jax
import jax.numpy as jnp
from jax import lax
from jax.experimental import pallas as pl
from jax.experimental.pallas import tpu as pltpu
from jax.sharding import PartitionSpec as P

MESH = pl.DeviceIdType.MESH
F32 = jnp.float32
BF16 = jnp.bfloat16

SEQ = 512
SITES = 8
WIDTH = 256
PROJ = 32
PAIR = 128
NDEV = 128
CHUNK = 128
NCHUNK = SEQ // CHUNK
BLOCK = SITES * PROJ
SLOT = BLOCK + 16
HALF = 128
EARLY, PER = 4, 2


def place():
    g = lax.axis_index("grp")
    d = lax.axis_index("dev")
    return g, d


def coords(g, d):
    return (d // 2 % 2) * 2 + g % 2, d // 4, g // 2, d % 2


def remote(src, dst, send, recv, target):
    return pltpu.make_async_remote_copy(
        src_ref=src, dst_ref=dst, send_sem=send, recv_sem=recv, device_id=target, device_id_type=MESH
    )


def column(row):
    n = row.shape[1]
    a = lax.broadcasted_iota(jnp.int32, (n, n), 0)
    b = lax.broadcasted_iota(jnp.int32, (n, n), 1)
    return jnp.sum(jnp.where(a == b, jnp.broadcast_to(row, (n, n)), 0.0), axis=1, keepdims=True)


def kernel(
    x_hbm, marks_h, gain1_h, shift1_h, wl_h, bl_h, wr_h, br_h, wd_h, gain2_h, shift2_h,
    pair_out, row_hbm,
    marks, gain1, shift1, wl, bl, wr, br, wd, gain2, shift2,
    xv, nf, rowbuf, rf, lslot, rslot, ra, rt, mrt, wf, w2, xs,
    psem, xsem, lrecv, lrecv2, lsend, rrecv, rrecv2, rsend, asend, arecv, plane, cube,
):
    g, d = place()
    me = g * 16 + d
    x0, y0, z0, c0 = coords(g, d)
    xh0 = d // 2 % 2

    groups = [
        (z0 + dz) % 4 * 2 + (g + dx) % 2 for dx, dz in
        ((0, 1), (1, 3), (0, 3), (1, 1), (0, 2), (1, 2), (1, 0), (0, 0))
    ]

    def column_of(q):
        o = lax.rem(q, 4)
        u = lax.rem(lax.div(q, 4) + 1, 4)
        dy = 1 + 2 * o + lax.div(o, 2) * (5 - 4 * o)
        return (
            lax.rem(y0 + dy, 4) * 4
            + lax.rem(xh0 + lax.div(u, 2), 2) * 2
            + lax.rem(c0 + lax.rem(u, 2), 2)
        )

    def xcopy(k):
        return pltpu.make_async_copy(
            x_hbm.at[pl.ds(k * CHUNK, CHUNK)], xv.at[pl.ds(k * CHUNK, CHUNK)], xsem.at[k]
        )

    small = (
        (gain1_h, gain1), (shift1_h, shift1), (gain2_h, gain2), (shift2_h, shift2), (marks_h, marks),
        (wl_h, wl), (wr_h, wr), (bl_h, bl), (br_h, br), (wd_h, wd),
    )
    for k, (a, b) in enumerate(small):
        pltpu.make_async_copy(a, b, psem.at[k]).start()
    for k in range(NCHUNK):
        xcopy(k).start()

    def left_slot(dy, dxh, dc):
        return lax.rem(y0 + dy, 4) * 4 + lax.rem(xh0 + dxh, 2) * 2 + lax.rem(c0 + dc, 2)

    def right_slot(dz, dxl):
        return lax.rem(z0 + dz, 4) * 2 + lax.rem(g + dxl, 2)

    ring_y = [(g, left_slot(k, 0, 0)) for k in (1, 3, 2)]
    ring_z = [(right_slot(k, 0), d) for k in (1, 3, 2)]
    row_x = [
        (right_slot(0, k // 4), left_slot(0, k // 2 % 2, k % 2)) for k in range(1, 8)
    ]
    barrier = pltpu.get_barrier_semaphore()
    for to in row_x + ring_y + ring_z:
        pl.semaphore_signal(barrier, inc=1, device_id=to, device_id_type=MESH)

    for k, (a, b) in enumerate(small):
        pltpu.make_async_copy(a, b, psem.at[k]).wait()

    def norm(k, carry):
        xcopy(k).wait()
        x = xv[pl.ds(k * CHUNK, CHUNK)].astype(F32).reshape(CHUNK * SITES, WIDTH)
        mean = jnp.sum(x, axis=-1, keepdims=True) * (1.0 / WIDTH)
        cen = x - mean
        var = jnp.sum(cen * cen, axis=-1, keepdims=True) * (1.0 / WIDTH)
        scaled = cen * lax.rsqrt(var + 1e-05)
        rows = pl.ds(pl.multiple_of(k * CHUNK * SITES, CHUNK * SITES), CHUNK * SITES)
        rowbuf[rows, :] = (scaled * gain2[...] + shift2[...]).astype(BF16)
        normed = scaled * gain1[...] + shift1[...]
        nf[0, rows, :] = normed[:, :128]
        nf[1, rows, :] = normed[:, 128:]
        return carry

    lax.fori_loop(0, NCHUNK, norm, 0)

    pl.semaphore_wait(barrier, 13)
    for to in ring_y:
        pl.semaphore_signal(plane, inc=1, device_id=to, device_id_type=MESH)

    def send_rows(q, targets):
        td = column_of(q)
        for tg in targets:
            to = tg * 16 + td
            remote(
                rowbuf.at[pl.ds(pl.multiple_of(to * 32, 32), 32)],
                row_hbm.at[pl.ds(pl.multiple_of(me * 32, 32), 32)],
                asend, arecv, (tg, td),
            ).start()

    def send_level(q, carry):
        send_rows(q, groups[6:])
        return carry

    def send_across(q, carry):
        send_rows(q, groups[:6])
        return carry

    mine = pl.ds(pl.multiple_of(me * 32, 32), 32)
    pltpu.make_async_copy(rowbuf.at[mine], row_hbm.at[mine], arecv).start()

    wt = jnp.concatenate([wl[...], wr[...]], axis=0)
    bias = jnp.concatenate([column(bl[...]), column(br[...])], axis=0)
    mask = marks[...].astype(F32)
    mask16 = jnp.concatenate([mask, jnp.zeros_like(mask)], axis=0).astype(BF16)
    for i in range(SITES):
        rows = jnp.concatenate(
            [nf[0, pl.ds(i, SEQ, stride=SITES), :], nf[1, pl.ds(i, SEQ, stride=SITES), :]], axis=1
        ).astype(BF16)
        p = lax.dot_general(wt, rows, (((1,), (1,)), ((), ())), preferred_element_type=F32)
        p = (p + bias) * mask[i : i + 1, :]
        lslot[d, pl.ds(i * PROJ, PROJ), :] = p[:PROJ].astype(BF16)
        for h in range(4):
            rf[h, pl.ds(i, PROJ, stride=SITES), :] = p[PROJ:, h * 128 : (h + 1) * 128]
    for h in range(4):
        rslot[g, pl.ds(0, BLOCK), pl.ds(h * 128, 128)] = rf[h].astype(BF16)
    lslot[d, pl.ds(BLOCK, 16), :] = mask16
    rslot[g, pl.ds(BLOCK, 16), :] = mask16

    halves = (pl.ds(0, HALF), pl.ds(HALF, SLOT - HALF))
    lsems, rsems = (lrecv, lrecv2), (rrecv, rrecv2)
    here = (g, d)

    def left(slot, h, target):
        at = lslot.at[slot, halves[h]]
        return remote(at, at, lsend, lsems[h].at[slot], target)

    def right(slot, h, target):
        at = rslot.at[slot, halves[h]]
        return remote(at, at, rsend, rsems[h].at[slot], target)

    def whole(slot, target):
        return remote(lslot.at[slot], lslot.at[slot], lsend, lrecv.at[slot], target)

    sibling = (g, left_slot(0, 0, 1))
    lpartner = left_slot(0, 1, 0)
    rpartner = right_slot(0, 1)
    lup, ldown = (g, left_slot(1, 0, 0)), (g, left_slot(3, 0, 0))
    rup, rdown = (right_slot(1, 0), d), (right_slot(3, 0), d)

    def both_ways(send, slot, up, down):
        send(slot, 0, up).start()
        send(slot, 1, down).start()
        send(slot, 1, up).start()
        send(slot, 0, down).start()

    def onward(send, low, high, up, down):
        send(low, 0, here).wait_recv()
        send(low, 0, up).start()
        send(high, 1, here).wait_recv()
        send(high, 1, down).start()

    def share(k):
        low, high = left_slot(3, k, 0), left_slot(1, k, 0)
        left(low, 1, here).wait_recv()
        whole(low, sibling).start()
        left(high, 0, here).wait_recv()
        whole(high, sibling).start()

    def share_far(k):
        far = left_slot(2, k, 0)
        left(far, 0, here).wait_recv()
        left(far, 1, here).wait_recv()
        whole(far, sibling).start()

    right(g, 0, (rpartner, d)).start()
    right(g, 1, (rpartner, d)).start()
    left(d, 0, (g, lpartner)).start()
    left(d, 1, (g, lpartner)).start()
    both_ways(right, g, rup, rdown)
    both_ways(left, d, lup, ldown)
    whole(d, sibling).start()

    pl.semaphore_wait(plane, 3)
    for to in ring_z:
        pl.semaphore_signal(cube, inc=1, device_id=to, device_id_type=MESH)
    lax.fori_loop(0, 15, send_level, 0)
    send_rows(15, groups[6:7])

    right(rpartner, 0, here).wait_recv()
    right(rpartner, 0, rup).start()
    right(rpartner, 0, rdown).start()
    right(rpartner, 1, here).wait_recv()
    right(rpartner, 1, rdown).start()
    right(rpartner, 1, rup).start()
    onward(right, right_slot(3, 0), right_slot(1, 0), rup, rdown)
    onward(left, left_slot(3, 0, 0), left_slot(1, 0, 0), lup, ldown)
    share(0)
    onward(right, right_slot(3, 1), right_slot(1, 1), rup, rdown)
    left(lpartner, 0, here).wait_recv()
    left(lpartner, 0, lup).start()
    left(lpartner, 0, ldown).start()
    left(lpartner, 1, here).wait_recv()
    left(lpartner, 1, ldown).start()
    left(lpartner, 1, lup).start()
    whole(lpartner, sibling).start()
    pl.semaphore_wait(cube, 3)
    lax.fori_loop(0, EARLY, send_across, 0)
    share_far(0)

    wf[...] = wd[...].astype(F32)
    for e2 in range(2):
        stack = jnp.concatenate(
            [wf[pl.ds(2 * ep + e2, PROJ, stride=PROJ), :] for ep in range(PROJ // 2)], axis=0
        )
        w2[pl.ds(e2 * PAIR, PAIR), :] = stack.T.astype(BF16)

    for k in range(2):
        right(right_slot(3, k), 1, here).wait_recv()
        right(right_slot(1, k), 0, here).wait_recv()
        right(right_slot(2, k), 0, here).wait_recv()
        right(right_slot(2, k), 1, here).wait_recv()

    def merge(t, carry):
        e = pl.multiple_of(t * 4 * SITES, 4 * SITES)
        for q in range(4):
            a = rslot[2 * q, pl.ds(e, 4 * SITES), :].astype(F32).reshape(4, SITES, SEQ)
            b = rslot[2 * q + 1, pl.ds(e, 4 * SITES), :].astype(F32).reshape(4, SITES, SEQ)
            ra[:, pl.ds(q * 16, 16), :] = jnp.concatenate([a, b], axis=1).astype(BF16)
        for h in range(2):
            block = ra[2 * h : 2 * h + 2].reshape(128, SEQ)
            lanes = pl.ds(pl.multiple_of(t * 256 + h * 128, 128), 128)
            rt[:, lanes] = block.T
        return carry

    lax.fori_loop(0, PROJ // 4, merge, 0)
    mr = jnp.concatenate(
        [rslot[k, pl.ds(BLOCK, 16), :].astype(F32)[:SITES] for k in range(8)], axis=0
    )
    mrt[...] = jnp.concatenate([mr, mr], axis=0).astype(BF16).T

    low = lax.broadcasted_iota(jnp.int32, (1, 128), 1) < 64

    def outer(pair, buf):
        lhs = lslot[pl.ds(2 * pair, 2), pl.ds(0, BLOCK), :].reshape(2 * BLOCK, SEQ)
        for nb in range(8):
            x = jnp.dot(lhs, rt[:, nb * 256 : (nb + 1) * 256], preferred_element_type=F32).astype(BF16)
            for h in range(2):
                ep = nb * 2 + h
                for i in range(2 * SITES):
                    xs[buf, i, ep * PROJ : (ep + 1) * PROJ, :] = x[
                        i * PROJ : (i + 1) * PROJ, h * 128 : (h + 1) * 128
                    ]

    def combine(pair, buf):
        marks2 = lslot[pl.ds(2 * pair, 2), pl.ds(BLOCK, 16), :].reshape(32, SEQ)
        count = jnp.dot(marks2, mrt[...], preferred_element_type=F32)
        inverse = 1.0 / (count + 0.001)
        for i in range(0, 2 * SITES, 2):
            rhs = jnp.concatenate([xs[buf, i], xs[buf, i + 1]], axis=1)
            y = jnp.dot(w2[...], rhs, preferred_element_type=F32)
            a, b = y[:PAIR], y[PAIR:]
            early = a[:, :128] + pltpu.roll(b[:, :128], 64, axis=1)
            late = b[:, 128:] + pltpu.roll(a[:, 128:], 64, axis=1)
            both = jnp.where(low, early, late)
            m = i // SITES * 16 + i % SITES
            scale = jnp.where(low, inverse[m : m + 1], inverse[m + 1 : m + 2])
            at = pl.ds(pl.multiple_of(pair * 1024 + i * 64, 128), 128)
            pair_out[at, :] = (both * scale).astype(BF16).T

    def pair_at(t):
        o = lax.rem(t, 4)
        dy = o + lax.div(o, 2) * (5 - 2 * o)
        return lax.rem(y0 + dy, 4) * 2 + lax.rem(xh0 + lax.div(t, 4), 2)

    def await_sibling(t):
        whole(2 * pair_at(t) + 1 - c0, here).wait_recv()

    def step(t, carry):
        @pl.when(t == 1)
        def _():
            onward(left, left_slot(3, 1, 0), left_slot(1, 1, 0), lup, ldown)

        @pl.when(t == 2)
        def _():
            share(1)

        @pl.when(t == 3)
        def _():
            share_far(1)

        for k in range(PER):
            q = EARLY + (t - 1) * PER + k

            @pl.when(q < 16)
            def _():
                send_across(q, 0)

        await_sibling(t)
        now = lax.rem(t, 2)
        combine(pair_at(t - 1), 1 - now)
        outer(pair_at(t), now)
        return carry

    await_sibling(0)
    outer(pair_at(0), 0)
    lax.fori_loop(1, 8, step, 0)
    combine(pair_at(7), 1)

    pltpu.make_async_copy(lslot.at[pl.ds(0, 15)], lslot.at[pl.ds(0, 15)], lsend).wait()
    pltpu.make_async_copy(rslot.at[pl.ds(0, 7)], rslot.at[pl.ds(0, 7)], rsend).wait()
    rest = pl.ds(0, (NDEV - 1) * 32)
    pltpu.make_async_copy(rowbuf.at[rest], rowbuf.at[rest], asend).wait()
    pltpu.make_async_copy(rowbuf, row_hbm, arecv).wait()


def body(x, marks, gain1, shift1, wl, bl, wr, br, wd, gain2, shift2):
    hbm = pl.BlockSpec(memory_space=pltpu.HBM)
    free = pl.BlockSpec(memory_space=pl.ANY)
    pair, rows = pl.pallas_call(
        kernel,
        out_shape=(
            jax.ShapeDtypeStruct((8192, PAIR), BF16),
            jax.ShapeDtypeStruct((NDEV * 32, WIDTH), BF16),
        ),
        in_specs=[hbm] * 11,
        out_specs=(pl.BlockSpec(memory_space=pltpu.VMEM), free),
        scratch_shapes=[
            pltpu.VMEM((SITES, SEQ), jnp.int32),
            pltpu.VMEM((1, WIDTH), F32),
            pltpu.VMEM((1, WIDTH), F32),
            pltpu.VMEM((PROJ, WIDTH), BF16),
            pltpu.VMEM((1, PROJ), F32),
            pltpu.VMEM((PROJ, WIDTH), BF16),
            pltpu.VMEM((1, PROJ), F32),
            pltpu.VMEM((PROJ * PROJ, PAIR), BF16),
            pltpu.VMEM((1, WIDTH), F32),
            pltpu.VMEM((1, WIDTH), F32),
            pltpu.VMEM((SEQ, SITES, WIDTH), BF16),
            pltpu.VMEM((2, SEQ * SITES, 128), F32),
            pltpu.VMEM((SEQ * SITES, WIDTH), BF16),
            pltpu.VMEM((4, BLOCK, 128), F32),
            pltpu.VMEM((16, SLOT, SEQ), BF16),
            pltpu.VMEM((8, SLOT, SEQ), BF16),
            pltpu.VMEM((4, 64, SEQ), BF16),
            pltpu.VMEM((SEQ, 2048), BF16),
            pltpu.VMEM((SEQ, 128), BF16),
            pltpu.VMEM((PROJ * PROJ, PAIR), F32),
            pltpu.VMEM((2 * PAIR, 512), BF16),
            pltpu.VMEM((2, 2 * SITES, 512, 128), BF16),
            pltpu.SemaphoreType.DMA((10,)),
            pltpu.SemaphoreType.DMA((NCHUNK,)),
            pltpu.SemaphoreType.DMA((16,)),
            pltpu.SemaphoreType.DMA((16,)),
            pltpu.SemaphoreType.DMA,
            pltpu.SemaphoreType.DMA((8,)),
            pltpu.SemaphoreType.DMA((8,)),
            pltpu.SemaphoreType.DMA,
            pltpu.SemaphoreType.DMA,
            pltpu.SemaphoreType.DMA,
            pltpu.SemaphoreType.REGULAR,
            pltpu.SemaphoreType.REGULAR,
        ],
        compiler_params=pltpu.CompilerParams(
            collective_id=0, has_side_effects=True, vmem_limit_bytes=44 << 20
        ),
    )(
        *(
            pltpu.with_memory_space_constraint(v, pltpu.HBM)
            for v in (
                x, marks, gain1[None], shift1[None], wl.T, bl[None], wr.T, br[None], wd,
                gain2[None], shift2[None],
            )
        )
    )
    pair = pair.reshape(128, 8, 8, PAIR)
    rows = rows.reshape(NDEV, 4, SITES, WIDTH).transpose(1, 0, 2, 3).reshape(4, 1024, WIDTH)
    return pair, rows


def solution(mesh):
    everywhere = P()
    return jax.shard_map(
        body,
        mesh=mesh,
        in_specs=(P(None, ("grp", "dev"), None), P(("grp", "dev"), None)) + (everywhere,) * 9,
        out_specs=(P("grp", None, "dev", None), P(("grp", "dev"), None, None)),
        check_vma=False,
    )
```
